256 devices in a mesh: dp: 32 (over z, y_lo, core), grp: 8 (over x, y_hi).
Axes of the slice: x: 4, y: 4 (y_hi: 2, y_lo: 2; y = y_hi * 2 + y_lo), z: 8, core: 2. Of those that a mesh axis runs over, the one named last changes fastest.
Arguments:
- hidden_acts: bfloat16 [4, 16384, 11008], P(None, 'dp', 'grp'), may hold values from -30 to 30
- out_grads: bfloat16 [4, 16384, 4096], P(None, 'dp', 'grp'), may hold values from -30 to 30
- weight_grad: bfloat16 [4, 11008, 4096], P(None, 'grp', 'dp'), may hold values from -6 to 6
- owner_a: int32 [4, 64], P(None, 'grp'), may hold values from 0 to 31, as said below
- gradient_block_owner: int32 [4, 32], P(None, 'grp'), may hold values from 0 to 31, as said below
Outputs:
- precond_grad: bfloat16 [4, 11008, 4096], P(None, 'grp', 'dp')
- store_a: bfloat16 [8, 32, 2, 172, 172], P('grp', 'dp')
- store_g: bfloat16 [8, 32, 2, 128, 128], P('grp', 'dp')
The draws below stay inside these ranges and needn't reach their ends.
Inputs may be any that keep to these rules, and one draw needn't show every extreme that they name: `owner_a`: within the blocks of one grp index (all layers together), each dp index owns at most 2 input-side blocks, and one owns exactly 2. `gradient_block_owner`: within the blocks of one grp index (all layers together), each dp index owns at most 2 output-side blocks, and one owns exactly 2.
All inputs are finite; a program needn't handle non-finite values.
Results may differ from the reference program's by a relative error of at most 0.0064.
Values may be sent and summed in bfloat16 or wider, within the bound.
No kernel may reach another device: no remote copies, remote signals or barrier semaphores. Data moves between devices by JAX's collectives and lax.ppermute only.
A program may use at most 128 MiB of HBM per device.

```python
import math
import jax
import jax.numpy as jnp
from jax import lax

D = 4096
FF = 11008
LAYERS = 4
ITERS = 12
BA = 172
BG = 128
NBA = 64
NBG = 32
TOKENS = 16384
SLOTS_A = 2
SLOTS_G = 2
N_DP = 32
N_GRP = 8


def mixed_features(noise, scales):
    return (noise[..., :-3] + 0.6 * noise[..., 1:-2] - 0.4 * noise[..., 3:]) * scales


def feature_draw(key, width):
    key_noise, key_scale = jax.random.split(key, 2)
    shape = (LAYERS, TOKENS, width + 3)
    noise = jax.random.truncated_normal(key_noise, -4.0, 4.0, shape, jnp.float32)
    scales = jnp.exp(jax.random.uniform(key_scale, (width,), jnp.float32, math.log(0.3), math.log(3.0)))
    return mixed_features(noise, scales).astype(jnp.bfloat16)


def draw_hidden_acts(key, part):
    key = jax.random.fold_in(key, 11)
    return feature_draw(key, FF)


def draw_out_grads(key, part):
    key = jax.random.fold_in(key, 12)
    return feature_draw(key, D)


def spread_owners(key, per_layer, block_slots):
    per_column = per_layer // N_GRP
    column_blocks = LAYERS * per_column

    def one_column(column_key):
        key_order, key_rest, key_final = jax.random.split(column_key, 3)
        order = jax.random.permutation(key_order, N_DP).astype(jnp.int32)
        others = jax.random.permutation(key_rest, jnp.repeat(order[1:], block_slots))
        tickets = jnp.concatenate([jnp.full((block_slots,), order[0], jnp.int32), others])[:column_blocks]
        return jax.random.permutation(key_final, tickets)
    columns = jax.vmap(one_column)(jax.random.split(key, N_GRP))
    return columns.reshape(N_GRP, LAYERS, per_column).transpose(1, 0, 2).reshape(LAYERS, per_layer).astype(jnp.int32)


def draw_owner_a(key, part):
    key = jax.random.fold_in(key, 21)
    return spread_owners(key, NBA, SLOTS_A)


def draw_gradient_block_owner(key, part):
    key = jax.random.fold_in(key, 22)
    return spread_owners(key, NBG, SLOTS_G)


def block_scale(key, shape, cuts, least, high):
    def one(axis_at, shards_of):
        draws = jax.random.uniform(jax.random.fold_in(jax.random.fold_in(key, 6), axis_at), (shards_of,), jnp.float32, least / len(cuts), high / len(cuts))
        return jnp.repeat(jnp.exp(draws), shape[axis_at] // shards_of).reshape((-1,) + (1,) * (len(shape) - axis_at - 1))

    gain = one(*cuts[0])
    for cut in cuts[1:]:
        gain = gain * one(*cut)
    return gain


def gaussian(own_key, shape, spread, limit, cuts=(), kind=jnp.bfloat16):
    loudness = block_scale(own_key, shape, cuts, -0.22, 0.18) if cuts else 1.0
    array = jax.random.normal(own_key, shape, jnp.float32) * spread * loudness
    return jnp.minimum(jnp.maximum(array, -limit), limit).astype(kind)


def setup_inputs(seed: int = 0) -> dict:
    keys = jax.random.split(jax.random.key(seed), 6)
    hidden_acts = draw_hidden_acts(jax.random.fold_in(keys[5], 71), 0)
    out_grads = draw_out_grads(jax.random.fold_in(keys[5], 71), 0)
    weight_grad = gaussian(keys[2], (LAYERS, FF, D), 1.0, 6.0, ((1, 8), (2, 32)))
    owner_a = draw_owner_a(jax.random.fold_in(keys[5], 71), 0)
    gradient_block_owner = draw_gradient_block_owner(jax.random.fold_in(keys[5], 71), 0)
    return dict(hidden_acts=hidden_acts, out_grads=out_grads, weight_grad=weight_grad, owner_a=owner_a, gradient_block_owner=gradient_block_owner)


damping_share = 0.01

def inverse_roots(blocks, filler):
    width = blocks.shape[-1]
    identity = jnp.eye(width, dtype=jnp.float32)
    trace_raw = jnp.trace(blocks, axis1=1, axis2=2)
    damped = blocks + (damping_share * trace_raw / width + filler)[:, None, None] * identity
    total = jnp.trace(damped, axis1=1, axis2=2)
    start_y = damped / total[:, None, None]
    start_z = jnp.broadcast_to(identity, damped.shape)

    def sweep(index, carry):
        left_y, left_z = carry
        poly = 1.5 * identity - 0.5 * jnp.einsum('nij,njk->nik', left_z, left_y, precision=lax.Precision.HIGHEST)
        next_y = jnp.einsum('nij,njk->nik', left_y, poly, precision=lax.Precision.HIGHEST)
        next_z = jnp.einsum('nij,njk->nik', poly, left_z, precision=lax.Precision.HIGHEST)
        return (next_y, next_z)
    final_y, final_z = lax.fori_loop(0, ITERS, sweep, (start_y, start_z))
    return (final_z / jnp.sqrt(total)[:, None, None]).astype(jnp.bfloat16)

def owner_ranks(owners):
    places = jnp.arange(owners.shape[0], dtype=jnp.int32)
    same = owners[:, None] == owners[None, :]
    earlier = places[None, :] < places[:, None]
    return lax.optimization_barrier(jnp.sum(jnp.logical_and(same, earlier), axis=1)).astype(jnp.int32)

def covariance_blocks(acts, width):

    def one_layer(layer):
        blocks = layer.astype(jnp.float32).reshape(layer.shape[0], -1, width)
        return jnp.einsum('tkb,tkc->kbc', blocks, blocks, precision=lax.Precision.HIGHEST) * (1.0 / TOKENS)
    return lax.map(one_layer, acts)

def owner_store(roots, owners, block_slots):
    layers, blocks, width = (roots.shape[0], roots.shape[1], roots.shape[2])
    per_column = blocks // N_GRP
    col_roots = roots.reshape(layers, N_GRP, per_column, width, width).transpose(1, 0, 2, 3, 4)
    col_roots = col_roots.reshape(N_GRP, layers * per_column, width, width)
    col_owner = owners.reshape(layers, N_GRP, per_column).transpose(1, 0, 2).reshape(N_GRP, layers * per_column)

    def one_column(these_roots, these_owners):
        slot_indices = these_owners * block_slots + owner_ranks(these_owners)
        empty = jnp.zeros((N_DP * block_slots, width, width), jnp.bfloat16)
        return empty.at[slot_indices].set(these_roots)
    stores = jax.vmap(one_column)(col_roots, col_owner)
    return stores.reshape(N_GRP, N_DP, block_slots, width, width)

def reference(hidden_acts, out_grads, weight_grad, owner_a, gradient_block_owner):
    cov_a = covariance_blocks(hidden_acts, BA).reshape(LAYERS * NBA, BA, BA)
    cov_g = covariance_blocks(out_grads, BG).reshape(LAYERS * NBG, BG, BG)
    root_a = inverse_roots(cov_a, jnp.zeros((LAYERS * NBA,), jnp.float32)).reshape(LAYERS, NBA, BA, BA)
    root_g = inverse_roots(cov_g, jnp.zeros((LAYERS * NBG,), jnp.float32)).reshape(LAYERS, NBG, BG, BG)
    store_a = owner_store(root_a, owner_a, SLOTS_A)
    store_g = owner_store(root_g, gradient_block_owner, SLOTS_G)

    def one_layer(inputs):
        grad_layer, left_roots, right_roots = inputs
        tiles = grad_layer.astype(jnp.float32).reshape(NBA, BA, NBG, BG)
        mid = jnp.einsum('kajb,jbc->kajc', tiles, right_roots.astype(jnp.float32), precision=lax.Precision.HIGHEST)
        mid = mid.astype(jnp.bfloat16).astype(jnp.float32)
        result = jnp.einsum('kab,kbjc->kajc', left_roots.astype(jnp.float32), mid, precision=lax.Precision.HIGHEST)
        return result.astype(jnp.bfloat16).reshape(FF, D)
    precond_grad = lax.map(one_layer, (weight_grad, root_a, root_g))
    return (precond_grad, store_a, store_g)
```

```python
import functools

import jax
import jax.numpy as jnp
from jax import lax
from jax.experimental import pallas as pl
from jax.experimental.pallas import tpu as pltpu
from jax.sharding import PartitionSpec as P

ITERS = 12
BA = 172
BG = 128
LAYERS = 4
HALF = 64
NARROW = BA - BG
RA = 144
RG = 64
MSG = RA + RG
PAIR = RA + RG + RA
DIAG = 136
GATHERED = RA + RG // 2
TAIL = 128
WIRE = jnp.float16
WIRE_SCALE = 512.0

damping_share = 0.01

PARAMS = pltpu.CompilerParams(vmem_limit_bytes=48 << 20)


def iota(shape, dim):
    return lax.broadcasted_iota(jnp.int32, shape, dim)


def pack_square(top, bottom):
    row, lane = iota((HALF, BG), 0), iota((HALF, BG), 1)
    turned = pltpu.roll(bottom, HALF, 1)
    folded = jnp.where((lane < HALF) & (row >= lane), turned, top)
    diagonal = jnp.sum(jnp.where(row == lane, top, 0.0), axis=0, keepdims=True)
    return folded, diagonal


def unpack_square(folded, diagonal):
    row, lane = iota((HALF, BG), 0), iota((HALF, BG), 1)
    top = jnp.where(lane > row, folded, jnp.where(lane == row, 0.5 * diagonal, 0.0))
    left = jnp.where(lane < row, folded, jnp.where(lane == row, 0.5 * folded, 0.0))
    bottom = pltpu.roll(left, HALF, 1)
    once = jnp.concatenate([top, bottom], axis=0)
    return once + once.T


def pack_wide(full, spare):
    folded, diagonal = pack_square(full[0:HALF, 0:BG], full[HALF:BG, 0:BG])
    low = full[BG : BG + 48, 0:BG]
    corner = full[BG : BG + 48, BG:256]
    corner = corner[0:24] + pltpu.roll(corner[24:48], HALF, 1)
    both = diagonal + pltpu.roll(spare, HALF, 1)
    last = jnp.where(iota((8, BG), 0) == 0, both, 0.0)
    return folded, low, jnp.concatenate([corner, last], axis=0)


def unpack_wide(packed):
    square = unpack_square(packed[0:HALF], packed[DIAG : DIAG + 1])
    low = packed[HALF : HALF + 48]
    tall = jnp.concatenate([low, jnp.zeros((80, BG), jnp.float32)], axis=0).T
    corner = packed[112:136]
    lane, row = iota((24, BG), 1), iota((24, BG), 0)
    first = jnp.where(lane < NARROW, corner, 0.0)
    second = jnp.where((lane < NARROW) & (row < NARROW - 24), pltpu.roll(corner, HALF, 1), 0.0)
    corner = jnp.concatenate([first, second], axis=0)
    return jnp.concatenate(
        [jnp.concatenate([square, tall], axis=1), jnp.concatenate([low, corner], axis=1)], axis=0
    )


def cov_kernel(scale, sel_ref, h_ref, g_ref, o_ref, wide):
    wide[...] = jnp.zeros_like(wide)
    squares = []
    for m in range(4):
        x = g_ref[m]
        c = lax.dot_general(x, x, (((0,), (0,)), ((), ())), preferred_element_type=jnp.float32)
        squares.append(pack_square(c[0:HALF] * scale, c[HALF:BG] * scale))
    for k in range(8):
        x = h_ref[0, BA * k : BA * (k + 1), :]
        c = lax.dot_general(x, x, (((1,), (1,)), ((), ())), preferred_element_type=jnp.float32)
        wide[k, 0:BA, 0:BA] = c * scale
    z = sel_ref[1]
    for m in range(4):
        folded, spare = squares[m]
        o_ref[0, lax.rem(m - z + 8, 4), RA : RA + RG] = folded
        for k in (m, m + 4):
            shift = lax.rem(k - z + 8, 8)
            place, base = lax.rem(shift, 4), pl.multiple_of((shift // 4) * MSG, 16)
            folded, low, corner = pack_wide(wide.at[k], spare)
            o_ref[0, place, pl.ds(base, HALF)] = folded
            o_ref[0, place, pl.ds(base + HALF, 48)] = low
            o_ref[0, place, pl.ds(base + 112, 32)] = corner


def covariances(turned, grads, core, z, scale):
    rows, features = turned.shape[2], turned.shape[1]
    return pl.pallas_call(
        functools.partial(cov_kernel, scale),
        grid_spec=pltpu.PrefetchScalarGridSpec(
            num_scalar_prefetch=1,
            grid=(2,),
            in_specs=[
                pl.BlockSpec((1, features, rows), lambda i, s: (2 * s[0] + i, 0, 0)),
                pl.BlockSpec((LAYERS, rows, BG), lambda i, s: (0, 0, 2 * i + s[0])),
            ],
            out_specs=pl.BlockSpec((1, 4, PAIR, BG), lambda i, s: (i, 0, 0, 0)),
            scratch_shapes=[pltpu.VMEM((8, 176, 256), jnp.float32)],
        ),
        out_shape=jax.ShapeDtypeStruct((2, 4, PAIR, BG), jnp.float32),
        compiler_params=PARAMS,
        cost_estimate=pl.CostEstimate(flops=2 * 10**9, bytes_accessed=6 * 10**6, transcendentals=0),
        name="covariances",
    )(jnp.stack([core, z]), turned, grads)


def parts_of(x):
    high = x.astype(jnp.bfloat16)
    return high, (x - high.astype(jnp.float32)).astype(jnp.bfloat16)


def times(a, b):
    def one(i, j):
        return jnp.dot(a[i], b[j], preferred_element_type=jnp.float32)

    return (one(0, 1) + one(1, 0)) + one(0, 0)


def roots_kernel(z_ref, total_ref, packed_ref, wide, square):
    total = total_ref[...]
    spare = pltpu.roll(total[DIAG : DIAG + 1], HALF, 1)
    blocks = [unpack_wide(total[0:RA])[0:BA, 0:BA], unpack_square(total[RA:MSG], spare)]
    eyes, ys, totals = [], [], []
    for c in blocks:
        width = c.shape[0]
        eye = (iota(c.shape, 0) == iota(c.shape, 1)).astype(jnp.float32)
        damped = c + (damping_share * jnp.sum(c * eye) / width) * eye
        trace = jnp.sum(damped * eye)
        eyes.append(eye)
        ys.append(damped / trace)
        totals.append(trace)
    both = range(2)
    zs = [1.5 * eyes[i] - 0.5 * ys[i] for i in both]
    ys = [times(parts_of(ys[i]), parts_of(zs[i])) for i in both]

    def sweep(_, carry):
        ys, zs = carry
        sy, sz = [parts_of(y) for y in ys], [parts_of(z) for z in zs]
        sp = [parts_of(1.5 * eyes[i] - 0.5 * times(sz[i], sy[i])) for i in both]
        return [times(sy[i], sp[i]) for i in both], [times(sp[i], sz[i]) for i in both]

    ys, zs = lax.fori_loop(0, ITERS - 2, sweep, (ys, zs))
    sz = [parts_of(z) for z in zs]
    sp = [parts_of(1.5 * eyes[i] - 0.5 * times(sz[i], parts_of(ys[i]))) for i in both]
    roots = [times(sp[i], sz[i]) / jnp.sqrt(totals[i]) for i in both]
    wide[...] = jnp.zeros_like(wide)
    wide[0:BA, 0:BA] = roots[0]
    square[...], spare = pack_square(roots[1][0:HALF], roots[1][HALF:BG])
    folded, low, corner = pack_wide(wide, spare)
    packed_ref[0:HALF] = folded.astype(jnp.bfloat16)
    packed_ref[HALF:112] = low.astype(jnp.bfloat16)
    packed_ref[112:RA] = corner.astype(jnp.bfloat16)
    start = pl.multiple_of((z_ref[0] // 4) * (RG // 2), RG // 2)
    packed_ref[RA:GATHERED] = square[pl.ds(start, RG // 2)].astype(jnp.bfloat16)


def inverse_roots(total, z):
    whole = pl.BlockSpec(memory_space=pltpu.VMEM)
    return pl.pallas_call(
        roots_kernel,
        in_specs=[pl.BlockSpec(memory_space=pltpu.SMEM), whole],
        out_specs=whole,
        out_shape=jax.ShapeDtypeStruct((GATHERED, BG), jnp.bfloat16),
        scratch_shapes=[pltpu.VMEM((176, 256), jnp.float32), pltpu.VMEM((RG, BG), jnp.float32)],
        compiler_params=PARAMS,
        name="inverse_roots",
    )(z.reshape(1), total)


def unpack_halves(first, second):
    folded = jnp.concatenate([first[16:48], second[16:48]], axis=0)
    return unpack_square(folded, pltpu.roll(first[DIAG - TAIL : DIAG - TAIL + 1], HALF, 1))


def apply_kernel(at_ref, w_ref, a_ref, rights_ref, out_ref, sa_ref, sg_ref, right, mid):
    z, y, c, g = (at_ref[i] for i in range(4))

    def place(z_of, y_of, c_of):
        away = lax.rem(z - z_of + 8, 8)
        middle = (away == 0) | (away == 4)
        holder = jnp.where(middle, c_of, (away > 4).astype(jnp.int32))
        step = jnp.where(away > 4, 8 - away, away)
        slot = jnp.where(middle, 7 * (away // 4), 2 * step - 1 + jnp.bitwise_xor(c_of, holder))
        return jnp.bitwise_xor(holder, c), jnp.bitwise_xor(y_of, y), slot

    for d in range(8):
        right[lax.rem(g - (1 - 2 * c) * d + 8, 8)] = rights_ref[d].astype(jnp.float32)
    for layer in range(LAYERS):
        root = unpack_halves(right[layer], right[layer + 4]).astype(jnp.bfloat16)
        product = jnp.dot(w_ref[layer], root, preferred_element_type=jnp.float32)
        mid[layer] = product.astype(jnp.bfloat16).astype(jnp.float32)
        for quad in range(2):
            results = []
            for k in range(4 * quad, 4 * quad + 4):
                i, j, slot = place(k, layer % 2, layer // 2)
                left = unpack_wide(a_ref[i, j, slot, 0:RA].astype(jnp.float32))
                left = left[0:BA, 0:BA].astype(jnp.bfloat16)
                x = mid[layer, BA * k : BA * (k + 1)].astype(jnp.bfloat16)
                results.append(jnp.dot(left, x, preferred_element_type=jnp.float32))
            out_ref[layer, 4 * BA * quad : 4 * BA * (quad + 1)] = jnp.concatenate(
                results, axis=0
            ).astype(jnp.bfloat16)
    for r in range(2):
        block = at_ref[4 + r]
        held = jnp.maximum(block, 0)
        layer = held // 8
        i, j, slot = place(lax.rem(held, 8), lax.rem(layer, 2), layer // 2)
        root = unpack_wide(a_ref[i, j, slot, 0:RA].astype(jnp.float32))[0:BA, 0:BA]
        sa_ref[r] = jnp.where(block >= 0, root, 0.0).astype(jnp.bfloat16)
        block = at_ref[6 + r]
        held = jnp.maximum(block, 0)
        layer, k = held // 4, lax.rem(held, 4)
        halves = []
        for half in range(2):
            i, j, slot = place(layer + 4 * half, k // 2, lax.rem(k, 2))
            halves.append(a_ref[i, j, slot, TAIL:GATHERED].astype(jnp.float32))
        root = unpack_halves(*halves)
        sg_ref[r] = jnp.where(block >= 0, root, 0.0).astype(jnp.bfloat16)


def apply_roots(at, weight_grad, lefts, rights):
    whole = pl.BlockSpec(memory_space=pltpu.VMEM)
    rows = weight_grad.shape[1]
    return pl.pallas_call(
        apply_kernel,
        in_specs=[pl.BlockSpec(memory_space=pltpu.SMEM)] + [whole] * 3,
        out_specs=[whole] * 3,
        out_shape=[
            jax.ShapeDtypeStruct(weight_grad.shape, jnp.bfloat16),
            jax.ShapeDtypeStruct((2, BA, BA), jnp.bfloat16),
            jax.ShapeDtypeStruct((2, BG, BG), jnp.bfloat16),
        ],
        scratch_shapes=[
            pltpu.VMEM((8, GATHERED - TAIL, BG), jnp.float32),
            pltpu.VMEM((LAYERS, rows, BG), jnp.float32),
        ],
        compiler_params=PARAMS,
        name="apply_roots",
    )(at, weight_grad, lefts, rights)


def owned_blocks(owners, position):
    flat = owners.reshape(-1)
    mine = flat == position
    rank = jnp.cumsum(mine.astype(jnp.int32)) - 1
    places = jnp.arange(flat.shape[0], dtype=jnp.int32)
    return [jnp.max(jnp.where(mine & (rank == r), places, -1)) for r in range(2)]


def along_z(shift, away=False):
    return [(i, (i + 4 * shift * (1 - 2 * (i % 2) if away else 1)) % 32) for i in range(32)]


OVER_CORE = [(i, i ^ 1) for i in range(32)]
OVER_Y = [(i, i ^ 2) for i in range(32)]
EXCHANGE = [
    ((z * 4 + r) * 8 + g, (g * 4 + r) * 8 + z) for z in range(8) for r in range(4) for g in range(8)
]


def narrow(x):
    return (x * WIRE_SCALE).astype(WIRE)


def widen(x):
    return x.astype(jnp.float32) * (1.0 / WIRE_SCALE)


def shards(hidden_acts, out_grads, weight_grad, owner_a, gradient_block_owner):
    position = lax.axis_index("dp")
    column = lax.axis_index("grp")
    z, y, core = position // 4, lax.rem(position // 2, 2), lax.rem(position, 2)
    scale = 1.0 / (hidden_acts.shape[1] * lax.axis_size("dp"))
    turned = jnp.swapaxes(hidden_acts, 1, 2)

    theirs = covariances(turned, out_grads, 1 - core, z, scale)
    got = lax.ppermute(theirs, "dp", OVER_CORE)
    mine = covariances(turned, out_grads, core, z, scale)

    def summed(at):
        one = lax.dynamic_index_in_dim(mine, at, 0, False)
        return one + lax.dynamic_index_in_dim(got, at, 0, False)

    got_y = lax.ppermute(narrow(summed(1 - y)), "dp", OVER_Y)
    kept = summed(y) + widen(got_y)

    def message(s):
        a = kept[s % 4, (s // 4) * MSG : (s // 4) * MSG + RA]
        return jnp.concatenate([a, kept[s % 4, RA:MSG]], axis=0)

    arrived = [lax.ppermute(narrow(message(s)), "dp", along_z(s)) for s in range(1, 8)]
    total = message(0) + sum(widen(x) for x in arrived)
    packed = inverse_roots(total, z)

    pair = jnp.stack([packed, lax.ppermute(packed, "dp", OVER_CORE)])
    near = [lax.ppermute(pair, "dp", along_z(s, True)) for s in range(1, 4)]
    far = lax.ppermute(packed, "dp", along_z(4))
    held = jnp.concatenate([packed[None], *near, far[None]])
    others = lax.ppermute(jnp.stack([x[1, TAIL:] for x in near]), "dp", OVER_CORE)
    tails = [packed[TAIL:]] + [x[0, TAIL:] for x in near] + [far[TAIL:]]
    tails = jnp.stack(tails + [others[2], others[1], others[0]])
    rights = lax.ppermute(tails, ("dp", "grp"), EXCHANGE)
    lefts = jnp.stack([held, lax.ppermute(held, "dp", OVER_Y)])
    lefts = jnp.stack([lefts, lax.ppermute(lefts, "dp", OVER_CORE)])

    at = jnp.stack(
        [z, y, core, column]
        + owned_blocks(owner_a, position)
        + owned_blocks(gradient_block_owner, position)
    ).astype(jnp.int32)
    precond_grad, store_a, store_g = apply_roots(at, weight_grad, lefts, rights)
    return precond_grad, store_a[None, None], store_g[None, None]


def solution(mesh):
    return jax.shard_map(
        shards,
        mesh=mesh,
        in_specs=(
            P(None, "dp", "grp"),
            P(None, "dp", "grp"),
            P(None, "grp", "dp"),
            P(None, "grp"),
            P(None, "grp"),
        ),
        out_specs=(
            P(None, "grp", "dp"),
            P("grp", "dp", None, None, None),
            P("grp", "dp", None, None, None),
        ),
        check_vma=False,
    )
```

```python
import functools

import jax
import jax.numpy as jnp
from jax import lax
from jax.experimental import pallas as pl
from jax.experimental.pallas import tpu as pltpu
from jax.sharding import PartitionSpec as P

ITERS = 12
BA = 172
BG = 128
LAYERS = 4
HALF = 64
NARROW = BA - BG
RA = 144
RG = 64
MSG = RA + RG
PAIR = RA + RG + RA
DIAG = 136
GATHERED = RA + RG // 2
TAILS = 144
WIRE = jnp.float16
WIRE_SCALE = 256.0

damping_share = 0.01

CHEAP = pl.CostEstimate(flops=10**4, bytes_accessed=10**4, transcendentals=0)
PARAMS = pltpu.CompilerParams(vmem_limit_bytes=48 << 20)


def iota(shape, dim):
    return lax.broadcasted_iota(jnp.int32, shape, dim)


def pack_square(top, bottom):
    row, lane = iota((HALF, BG), 0), iota((HALF, BG), 1)
    turned = pltpu.roll(bottom, HALF, 1)
    folded = jnp.where((lane < HALF) & (row >= lane), turned, top)
    diagonal = jnp.sum(jnp.where(row == lane, top, 0.0), axis=0, keepdims=True)
    return folded, diagonal


def unpack_square(folded, diagonal):
    row, lane = iota((HALF, BG), 0), iota((HALF, BG), 1)
    top = jnp.where(lane > row, folded, jnp.where(lane == row, 0.5 * diagonal, 0.0))
    left = jnp.where(lane < row, folded, jnp.where(lane == row, 0.5 * folded, 0.0))
    bottom = pltpu.roll(left, HALF, 1)
    once = jnp.concatenate([top, bottom], axis=0)
    return once + once.T


def pack_wide(full, spare):
    folded, diagonal = pack_square(full[0:HALF, 0:BG], full[HALF:BG, 0:BG])
    low = full[BG : BG + 48, 0:BG]
    corner = full[BG : BG + 48, BG:256]
    corner = corner[0:24] + pltpu.roll(corner[24:48], HALF, 1)
    both = diagonal + pltpu.roll(spare, HALF, 1)
    last = jnp.where(iota((8, BG), 0) == 0, both, 0.0)
    return folded, low, jnp.concatenate([corner, last], axis=0)


def unpack_wide(packed):
    square = unpack_square(packed[0:HALF], packed[DIAG : DIAG + 1])
    low = packed[HALF : HALF + 48]
    tall = jnp.concatenate([low, jnp.zeros((80, BG), jnp.float32)], axis=0).T
    corner = packed[112:136]
    lane, row = iota((24, BG), 1), iota((24, BG), 0)
    first = jnp.where(lane < NARROW, corner, 0.0)
    second = jnp.where((lane < NARROW) & (row < NARROW - 24), pltpu.roll(corner, HALF, 1), 0.0)
    corner = jnp.concatenate([first, second], axis=0)
    return jnp.concatenate(
        [jnp.concatenate([square, tall], axis=1), jnp.concatenate([low, corner], axis=1)], axis=0
    )


def cov_kernel(scale, at_ref, h_ref, g_ref, o_ref, wide):
    z = at_ref[1]
    spares = []
    for layer in range(LAYERS):
        x = g_ref[layer]
        c = lax.dot_general(x, x, (((0,), (0,)), ((), ())), preferred_element_type=jnp.float32)
        folded, spare = pack_square(c[0:HALF] * scale, c[HALF:BG] * scale)
        spares.append(spare)
        turn = lax.rem(layer // 2 - z // 2 + 4, 2)
        o_ref[0, lax.rem(layer - z + 8, 2), turn, RA : RA + RG] = folded
    for k in range(8):
        x = h_ref[0, BA * k : BA * (k + 1), :]
        c = lax.dot_general(x, x, (((1,), (1,)), ((), ())), preferred_element_type=jnp.float32)
        wide[k, BG:176] = jnp.zeros((48, 256), jnp.float32)
        wide[k, 0:BA, 0:BA] = c * scale
    for k in range(8):
        turn = lax.rem(k // 2 - z // 2 + 4, 4)
        odd, place = lax.rem(k - z + 8, 2), lax.rem(turn, 2)
        base = pl.multiple_of((turn // 2) * MSG, 16)
        folded, low, corner = pack_wide(wide.at[k], spares[k % 4])
        o_ref[0, odd, place, pl.ds(base, HALF)] = folded
        o_ref[0, odd, place, pl.ds(base + HALF, 48)] = low
        o_ref[0, odd, place, pl.ds(base + 112, 32)] = corner


def covariances(turned, grads, core, z, scale):
    rows, features = turned.shape[2], turned.shape[1]
    shape = (2, 2, 2, PAIR, BG)
    return pl.pallas_call(
        functools.partial(cov_kernel, scale),
        grid_spec=pltpu.PrefetchScalarGridSpec(
            num_scalar_prefetch=1,
            grid=(2,),
            in_specs=[
                pl.BlockSpec((1, features, rows), lambda i, s: (2 * s[0] + i, 0, 0)),
                pl.BlockSpec((LAYERS, rows, BG), lambda i, s: (0, 0, 2 * i + s[0])),
            ],
            out_specs=pl.BlockSpec((1,) + shape[1:], lambda i, s: (i, 0, 0, 0, 0)),
            scratch_shapes=[pltpu.VMEM((8, 176, 256), jnp.float32)],
        ),
        out_shape=jax.ShapeDtypeStruct(shape, jnp.float32),
        compiler_params=PARAMS,
        cost_estimate=CHEAP,
        name="covariances",
    )(jnp.stack([core, z]), turned, grads)


def parts_of(x):
    high = x.astype(jnp.bfloat16)
    return high, (x - high.astype(jnp.float32)).astype(jnp.bfloat16)


def times(a, b):
    def one(i, j):
        return jnp.dot(a[i], b[j], preferred_element_type=jnp.float32)

    return (one(0, 1) + one(1, 0)) + one(0, 0)


def roots_kernel(z_ref, total_ref, packed_ref, wide, square):
    total = total_ref[...]
    spare = pltpu.roll(total[DIAG : DIAG + 1], HALF, 1)
    blocks = [unpack_wide(total[0:RA])[0:BA, 0:BA], unpack_square(total[RA:MSG], spare)]
    eyes, ys, totals = [], [], []
    for c in blocks:
        width = c.shape[0]
        eye = (iota(c.shape, 0) == iota(c.shape, 1)).astype(jnp.float32)
        damped = c + (damping_share * jnp.sum(c * eye) / width) * eye
        trace = jnp.sum(damped * eye)
        eyes.append(eye)
        ys.append(damped / trace)
        totals.append(trace)
    both = range(2)
    zs = [1.5 * eyes[i] - 0.5 * ys[i] for i in both]
    ys = [times(parts_of(ys[i]), parts_of(zs[i])) for i in both]

    def sweep(_, carry):
        ys, zs = carry
        sy, sz = [parts_of(y) for y in ys], [parts_of(z) for z in zs]
        sp = [parts_of(1.5 * eyes[i] - 0.5 * times(sz[i], sy[i])) for i in both]
        return [times(sy[i], sp[i]) for i in both], [times(sp[i], sz[i]) for i in both]

    ys, zs = lax.fori_loop(0, ITERS - 2, sweep, (ys, zs))
    sz = [parts_of(z) for z in zs]
    sp = [parts_of(1.5 * eyes[i] - 0.5 * times(sz[i], parts_of(ys[i]))) for i in both]
    roots = [times(sp[i], sz[i]) / jnp.sqrt(totals[i]) for i in both]
    wide[...] = jnp.zeros_like(wide)
    wide[0:BA, 0:BA] = roots[0]
    square[...], spare = pack_square(roots[1][0:HALF], roots[1][HALF:BG])
    folded, low, corner = pack_wide(wide, spare)
    packed_ref[0:HALF] = folded.astype(jnp.bfloat16)
    packed_ref[HALF:112] = low.astype(jnp.bfloat16)
    packed_ref[112:RA] = corner.astype(jnp.bfloat16)
    start = pl.multiple_of((z_ref[0] // 4) * (RG // 2), RG // 2)
    packed_ref[RA:GATHERED] = square[pl.ds(start, RG // 2)].astype(jnp.bfloat16)


def inverse_roots(total, z):
    whole = pl.BlockSpec(memory_space=pltpu.VMEM)
    return pl.pallas_call(
        roots_kernel,
        in_specs=[pl.BlockSpec(memory_space=pltpu.SMEM), whole],
        out_specs=whole,
        out_shape=jax.ShapeDtypeStruct((GATHERED, BG), jnp.bfloat16),
        scratch_shapes=[pltpu.VMEM((176, 256), jnp.float32), pltpu.VMEM((RG, BG), jnp.float32)],
        compiler_params=PARAMS,
        cost_estimate=CHEAP,
        name="inverse_roots",
    )(z.reshape(1), total)


def unpack_halves(first, second, spare):
    return unpack_square(jnp.concatenate([first, second], axis=0), pltpu.roll(spare, HALF, 1))


def owned_blocks(owners_ref, per_layer, position):
    first = second = jnp.int32(-1)
    for place in range(LAYERS * per_layer):
        mine = owners_ref[place // per_layer, place % per_layer] == position
        second = jnp.where(mine & (first >= 0), place, second)
        first = jnp.where(mine & (first < 0), place, first)
    return first, second


def right_kernel(g_ref, w_ref, even_ref, odd_ref, mid_ref, right, spares):
    for odd, ref in enumerate((even_ref, odd_ref)):
        for turn in range(4):
            source = lax.rem(jnp.bitwise_xor(g_ref[0], odd) - 2 * turn + 8, 8)
            right[source] = ref[32 * turn : 32 * (turn + 1)].astype(jnp.float32)
            spares[source] = ref[128:144].astype(jnp.float32)[turn : turn + 1]
    for layer in range(LAYERS):
        root = unpack_halves(right[layer], right[layer + 4], spares[layer]).astype(jnp.bfloat16)
        product = jnp.dot(w_ref[layer], root, preferred_element_type=jnp.float32)
        mid_ref[layer] = product.astype(jnp.bfloat16).astype(jnp.float32)


def multiply_right(column, weight_grad, even, odd):
    whole = pl.BlockSpec(memory_space=pltpu.VMEM)
    return pl.pallas_call(
        right_kernel,
        in_specs=[pl.BlockSpec(memory_space=pltpu.SMEM)] + [whole] * 3,
        out_specs=whole,
        out_shape=jax.ShapeDtypeStruct(weight_grad.shape, jnp.float32),
        scratch_shapes=[
            pltpu.VMEM((8, RG // 2, BG), jnp.float32),
            pltpu.VMEM((8, 1, BG), jnp.float32),
        ],
        compiler_params=PARAMS,
        cost_estimate=pl.CostEstimate(
            flops=2 * 10**10, bytes_accessed=6 * 10**6, transcendentals=0
        ),
        name="multiply_right",
    )(column, weight_grad, even, odd)


def apply_kernel(
    at_ref, oa_ref, og_ref, mid_ref, own_ref, beside_ref, out_ref, sa_ref, sg_ref, a_ref
):
    z, y, c = (at_ref[i] for i in range(3))
    position = 4 * z + 2 * y + c
    owned_a, owned_g = owned_blocks(oa_ref, 8, position), owned_blocks(og_ref, 4, position)

    def place(z_of, y_of, c_of):
        odd = lax.rem(z - z_of + 8, 2)
        start = jnp.where(odd == 1, jnp.bitwise_xor(z, 1), z)
        turn = lax.rem(start - z_of + 8, 8) // 2
        return jnp.bitwise_xor(c_of, c), 4 * (2 * odd + jnp.bitwise_xor(y_of, y)) + turn

    for i, ref in enumerate((own_ref, beside_ref)):
        for slot in range(16):
            a_ref[i, slot] = ref[GATHERED * slot : GATHERED * (slot + 1)]
    for layer in range(LAYERS):
        for quad in range(2):
            results = []
            for k in range(4 * quad, 4 * quad + 4):
                i, slot = place(k, layer % 2, layer // 2)
                left = unpack_wide(a_ref[i, slot, 0:RA].astype(jnp.float32))
                left = left[0:BA, 0:BA].astype(jnp.bfloat16)
                x = mid_ref[layer, BA * k : BA * (k + 1)].astype(jnp.bfloat16)
                results.append(jnp.dot(left, x, preferred_element_type=jnp.float32))
            out_ref[layer, 4 * BA * quad : 4 * BA * (quad + 1)] = jnp.concatenate(
                results, axis=0
            ).astype(jnp.bfloat16)
    stored = []
    for r in range(2):
        block = owned_a[r]
        held = jnp.maximum(block, 0)
        layer = held // 8
        i, slot = place(lax.rem(held, 8), lax.rem(layer, 2), layer // 2)
        root = unpack_wide(a_ref[i, slot, 0:RA].astype(jnp.float32))[0:BA, 0:BA]
        stored.append(jnp.where(block >= 0, root, 0.0))
        block = owned_g[r]
        held = jnp.maximum(block, 0)
        layer, k = held // 4, lax.rem(held, 4)
        halves = []
        for half in range(2):
            i, slot = place(layer + 4 * half, k // 2, lax.rem(k, 2))
            halves.append(a_ref[i, slot, RA - 16 : GATHERED].astype(jnp.float32))
        spare = halves[0][DIAG - RA + 16 : DIAG - RA + 17]
        root = unpack_halves(halves[0][16:48], halves[1][16:48], spare)
        sg_ref[r] = jnp.where(block >= 0, root, 0.0).astype(jnp.bfloat16)
    sa_ref[...] = jnp.stack(stored, axis=1).astype(jnp.bfloat16)


def apply_roots(at, owner_a, owner_g, mid, *gathered):
    whole = pl.BlockSpec(memory_space=pltpu.VMEM)
    return pl.pallas_call(
        apply_kernel,
        in_specs=[pl.BlockSpec(memory_space=pltpu.SMEM)] * 3 + [whole] * 3,
        out_specs=[whole] * 3,
        out_shape=[
            jax.ShapeDtypeStruct(mid.shape, jnp.bfloat16),
            jax.ShapeDtypeStruct((BA, 2, BA), jnp.bfloat16),
            jax.ShapeDtypeStruct((2, BG, BG), jnp.bfloat16),
        ],
        scratch_shapes=[pltpu.VMEM((2, 16, GATHERED, BG), jnp.bfloat16)],
        compiler_params=PARAMS,
        cost_estimate=CHEAP,
        name="apply_roots",
    )(at, owner_a, owner_g, mid, *gathered)


def along_z(shift):
    return [(i, (i + 4 * shift) % 32) for i in range(32)]


OVER_CORE = [(i, i ^ 1) for i in range(32)]
OVER_Y = [(i, i ^ 2) for i in range(32)]
OVER_Z = [(i, i ^ 4) for i in range(32)]
OVER_BOTH = [(i, i ^ 6) for i in range(32)]
EXCHANGE, EXCHANGE_ODD = (
    [
        ((z * 4 + r) * 8 + g, (g * 4 + (r ^ 1)) * 8 + (z ^ odd))
        for z in range(8)
        for r in range(4)
        for g in range(8)
    ]
    for odd in range(2)
)


def tails_of(messages):
    rows = [x[RA:GATHERED] for x in messages] + [x[DIAG : DIAG + 1] for x in messages]
    return jnp.concatenate(rows + [jnp.zeros((12, BG), jnp.bfloat16)])


def narrow(x):
    return (x * WIRE_SCALE).astype(WIRE)


def widen(x):
    return x.astype(jnp.float32) * (1.0 / WIRE_SCALE)


def shards(hidden_acts, out_grads, weight_grad, owner_a, gradient_block_owner):
    position = lax.axis_index("dp")
    column = lax.axis_index("grp")
    z, y, core = position // 4, lax.rem(position // 2, 2), lax.rem(position, 2)
    scale = 1.0 / (hidden_acts.shape[1] * lax.axis_size("dp"))
    turned = jnp.swapaxes(hidden_acts, 1, 2)

    theirs = covariances(turned, out_grads, 1 - core, z, scale)
    got = lax.ppermute(theirs, "dp", OVER_CORE)
    mine = covariances(turned, out_grads, core, z, scale)

    def chip_sum(of_y):
        one = lax.dynamic_index_in_dim(mine, of_y, 0, False)
        return one + lax.dynamic_index_in_dim(got, of_y, 0, False)

    other, own = chip_sum(1 - y), chip_sum(y)
    got_both = lax.ppermute(narrow(other[1]), "dp", OVER_BOTH)
    got_y = lax.ppermute(narrow(other[0]), "dp", OVER_Y)
    got_z = lax.ppermute(narrow(own[1]), "dp", OVER_Z)
    kept = (own[0] + widen(got_y)) + (widen(got_both) + widen(got_z))

    def message(turn):
        start = (turn // 2) * MSG
        return jnp.concatenate(
            [kept[turn % 2, start : start + RA], kept[turn % 2, RA:MSG]], axis=0
        )

    arrived = [lax.ppermute(narrow(message(t)), "dp", along_z(2 * t)) for t in range(1, 4)]
    total = message(0) + sum(widen(x) for x in arrived)
    packed = inverse_roots(total, z)

    held = [packed] + [lax.ppermute(packed, "dp", along_z(2 * t)) for t in range(1, 4)]
    tails = lax.ppermute(tails_of(held), "dp", OVER_CORE)
    held = jnp.concatenate(held)
    got_y = lax.ppermute(held, "dp", OVER_Y)
    got_z = lax.ppermute(held, "dp", OVER_Z)
    got_both = lax.ppermute(held, "dp", OVER_BOTH)
    tails = [lax.ppermute(tails, ("dp", "grp"), pairs) for pairs in (EXCHANGE, EXCHANGE_ODD)]
    gathered = jnp.concatenate([held, got_y, got_z, got_both])
    beside = lax.ppermute(gathered, "dp", OVER_CORE)

    at = jnp.stack([z, y, core])
    mid = multiply_right(column.reshape(1), weight_grad, *tails)
    precond_grad, store_a, store_g = apply_roots(
        at, owner_a, gradient_block_owner, mid, gathered, beside
    )
    return precond_grad, jnp.swapaxes(store_a, 0, 1)[None, None], store_g[None, None]


def solution(mesh):
    return jax.shard_map(
        shards,
        mesh=mesh,
        in_specs=(
            P(None, "dp", "grp"),
            P(None, "dp", "grp"),
            P(None, "grp", "dp"),
            P(None, "grp"),
            P(None, "grp"),
        ),
        out_specs=(
            P(None, "grp", "dp"),
            P("grp", "dp", None, None, None),
            P("grp", "dp", None, None, None),
        ),
        check_vma=False,
    )
```

```python
import functools

import jax
import jax.numpy as jnp
from jax import lax
from jax.experimental import pallas as pl
from jax.experimental.pallas import tpu as pltpu
from jax.sharding import PartitionSpec as P

ITERS = 12
BA = 172
BG = 128
LAYERS = 4
HALF = 64
NARROW = BA - BG
RA = 144
RG = 64
MSG = RA + RG
PAIR = RA + RG + RA
DIAG = 136
GATHERED = RA + RG // 2
TAILS = 144
WIRE = jnp.float16
WIRE_SCALE = 256.0

damping_share = 0.01

CHEAP = pl.CostEstimate(flops=10**4, bytes_accessed=10**4, transcendentals=0)
PARAMS = pltpu.CompilerParams(vmem_limit_bytes=48 << 20)


def iota(shape, dim):
    return lax.broadcasted_iota(jnp.int32, shape, dim)


def pack_square(top, bottom):
    row, lane = iota((HALF, BG), 0), iota((HALF, BG), 1)
    turned = pltpu.roll(bottom, HALF, 1)
    folded = jnp.where((lane < HALF) & (row >= lane), turned, top)
    diagonal = jnp.sum(jnp.where(row == lane, top, 0.0), axis=0, keepdims=True)
    return folded, diagonal


def unpack_square(folded, diagonal):
    row, lane = iota((HALF, BG), 0), iota((HALF, BG), 1)
    top = jnp.where(lane > row, folded, jnp.where(lane == row, 0.5 * diagonal, 0.0))
    left = jnp.where(lane < row, folded, jnp.where(lane == row, 0.5 * folded, 0.0))
    bottom = pltpu.roll(left, HALF, 1)
    once = jnp.concatenate([top, bottom], axis=0)
    return once + once.T


def pack_wide(full, spare):
    folded, diagonal = pack_square(full[0:HALF, 0:BG], full[HALF:BG, 0:BG])
    low = full[BG : BG + 48, 0:BG]
    corner = full[BG : BG + 48, BG:256]
    corner = corner[0:24] + pltpu.roll(corner[24:48], HALF, 1)
    both = diagonal + pltpu.roll(spare, HALF, 1)
    last = jnp.where(iota((8, BG), 0) == 0, both, 0.0)
    return folded, low, jnp.concatenate([corner, last], axis=0)


def unpack_wide(packed):
    square = unpack_square(packed[0:HALF], packed[DIAG : DIAG + 1])
    low = packed[HALF : HALF + 48]
    tall = jnp.concatenate([low, jnp.zeros((80, BG), jnp.float32)], axis=0).T
    corner = packed[112:136]
    lane, row = iota((24, BG), 1), iota((24, BG), 0)
    first = jnp.where(lane < NARROW, corner, 0.0)
    second = jnp.where((lane < NARROW) & (row < NARROW - 24), pltpu.roll(corner, HALF, 1), 0.0)
    corner = jnp.concatenate([first, second], axis=0)
    return jnp.concatenate(
        [jnp.concatenate([square, tall], axis=1), jnp.concatenate([low, corner], axis=1)], axis=0
    )


def cov_kernel(scale, at_ref, h_ref, g_ref, o_ref, wide):
    z = at_ref[1]
    spares = []
    for layer in range(LAYERS):
        x = g_ref[layer]
        c = lax.dot_general(x, x, (((0,), (0,)), ((), ())), preferred_element_type=jnp.float32)
        folded, spare = pack_square(c[0:HALF] * scale, c[HALF:BG] * scale)
        spares.append(spare)
        turn = (layer // 2 - (z >> 1)) & 1
        o_ref[0, (layer ^ z) & 1, turn, RA : RA + RG] = folded
    for k in range(8):
        x = h_ref[0, BA * k : BA * (k + 1), :]
        c = lax.dot_general(x, x, (((1,), (1,)), ((), ())), preferred_element_type=jnp.float32)
        wide[k, BG:176] = jnp.zeros((48, 256), jnp.float32)
        wide[k, 0:BA, 0:BA] = c * scale
    for k in range(8):
        turn = (k // 2 - (z >> 1)) & 3
        odd, place = (k ^ z) & 1, turn & 1
        base = pl.multiple_of((turn >> 1) * MSG, 16)
        folded, low, corner = pack_wide(wide.at[k], spares[k % 4])
        o_ref[0, odd, place, pl.ds(base, HALF)] = folded
        o_ref[0, odd, place, pl.ds(base + HALF, 48)] = low
        o_ref[0, odd, place, pl.ds(base + 112, 32)] = corner


def covariances(turned, grads, core, z, scale):
    rows, features = turned.shape[2], turned.shape[1]
    shape = (2, 2, 2, PAIR, BG)
    return pl.pallas_call(
        functools.partial(cov_kernel, scale),
        grid_spec=pltpu.PrefetchScalarGridSpec(
            num_scalar_prefetch=1,
            grid=(2,),
            in_specs=[
                pl.BlockSpec((1, features, rows), lambda i, s: (2 * s[0] + i, 0, 0)),
                pl.BlockSpec((LAYERS, rows, BG), lambda i, s: (0, 0, 2 * i + s[0])),
            ],
            out_specs=pl.BlockSpec((1,) + shape[1:], lambda i, s: (i, 0, 0, 0, 0)),
            scratch_shapes=[pltpu.VMEM((8, 176, 256), jnp.float32)],
        ),
        out_shape=jax.ShapeDtypeStruct(shape, jnp.float32),
        compiler_params=PARAMS,
        cost_estimate=CHEAP,
        name="covariances",
    )(jnp.stack([core, z]), turned, grads)


def parts_of(x):
    high = x.astype(jnp.bfloat16)
    return high, (x - high.astype(jnp.float32)).astype(jnp.bfloat16)


def times(a, b):
    def one(i, j):
        return jnp.dot(a[i], b[j], preferred_element_type=jnp.float32)

    return (one(0, 1) + one(1, 0)) + one(0, 0)


def roots_kernel(z_ref, total_ref, packed_ref, wide, square):
    total = total_ref[...]
    spare = pltpu.roll(total[DIAG : DIAG + 1], HALF, 1)
    blocks = [unpack_wide(total[0:RA])[0:BA, 0:BA], unpack_square(total[RA:MSG], spare)]
    eyes, ys, totals = [], [], []
    for c in blocks:
        width = c.shape[0]
        eye = (iota(c.shape, 0) == iota(c.shape, 1)).astype(jnp.float32)
        damped = c + (damping_share * jnp.sum(c * eye) / width) * eye
        trace = jnp.sum(damped * eye)
        eyes.append(eye)
        ys.append(damped / trace)
        totals.append(trace)
    both = range(2)
    zs = [1.5 * eyes[i] - 0.5 * ys[i] for i in both]
    ys = [times(parts_of(ys[i]), parts_of(zs[i])) for i in both]

    def sweep(_, carry):
        ys, zs = carry
        sy, sz = [parts_of(y) for y in ys], [parts_of(z) for z in zs]
        sp = [parts_of(1.5 * eyes[i] - 0.5 * times(sz[i], sy[i])) for i in both]
        return [times(sy[i], sp[i]) for i in both], [times(sp[i], sz[i]) for i in both]

    ys, zs = lax.fori_loop(0, ITERS - 2, sweep, (ys, zs))
    sz = [parts_of(z) for z in zs]
    sp = [parts_of(1.5 * eyes[i] - 0.5 * times(sz[i], parts_of(ys[i]))) for i in both]
    roots = [times(sp[i], sz[i]) / jnp.sqrt(totals[i]) for i in both]
    wide[...] = jnp.zeros_like(wide)
    wide[0:BA, 0:BA] = roots[0]
    square[...], spare = pack_square(roots[1][0:HALF], roots[1][HALF:BG])
    folded, low, corner = pack_wide(wide, spare)
    packed_ref[0:HALF] = folded.astype(jnp.bfloat16)
    packed_ref[HALF:112] = low.astype(jnp.bfloat16)
    packed_ref[112:RA] = corner.astype(jnp.bfloat16)
    start = pl.multiple_of((z_ref[0] >> 2) * (RG // 2), RG // 2)
    packed_ref[RA:GATHERED] = square[pl.ds(start, RG // 2)].astype(jnp.bfloat16)


def inverse_roots(total, z):
    whole = pl.BlockSpec(memory_space=pltpu.VMEM)
    return pl.pallas_call(
        roots_kernel,
        in_specs=[pl.BlockSpec(memory_space=pltpu.SMEM), whole],
        out_specs=whole,
        out_shape=jax.ShapeDtypeStruct((GATHERED, BG), jnp.bfloat16),
        scratch_shapes=[pltpu.VMEM((176, 256), jnp.float32), pltpu.VMEM((RG, BG), jnp.float32)],
        compiler_params=PARAMS,
        cost_estimate=CHEAP,
        name="inverse_roots",
    )(z.reshape(1), total)


def unpack_halves(first, second, spare):
    return unpack_square(jnp.concatenate([first, second], axis=0), pltpu.roll(spare, HALF, 1))


def owned_blocks(owners_ref, per_layer, position):
    first = second = jnp.int32(-1)
    for place in range(LAYERS * per_layer):
        mine = owners_ref[place // per_layer, place % per_layer] == position
        second = jnp.where(mine & (first >= 0), place, second)
        first = jnp.where(mine & (first < 0), place, first)
    return first, second


def right_kernel(at_ref, w_ref, even_ref, odd_ref, mid_ref, right, spares):
    start = source_of(at_ref[0], at_ref[1])
    for odd, ref in enumerate((even_ref, odd_ref)):
        for turn in range(4):
            source = ((start ^ odd) - 2 * turn) & 7
            right[source] = ref[32 * turn : 32 * (turn + 1)].astype(jnp.float32)
            spares[source] = ref[128:144].astype(jnp.float32)[turn : turn + 1]
    for layer in range(LAYERS):
        root = unpack_halves(right[layer], right[layer + 4], spares[layer]).astype(jnp.bfloat16)
        product = jnp.dot(w_ref[layer], root, preferred_element_type=jnp.float32)
        mid_ref[layer] = product.astype(jnp.bfloat16).astype(jnp.float32)


def multiply_right(at, weight_grad, even, odd):
    whole = pl.BlockSpec(memory_space=pltpu.VMEM)
    return pl.pallas_call(
        right_kernel,
        in_specs=[pl.BlockSpec(memory_space=pltpu.SMEM)] + [whole] * 3,
        out_specs=whole,
        out_shape=jax.ShapeDtypeStruct(weight_grad.shape, jnp.float32),
        scratch_shapes=[
            pltpu.VMEM((8, RG // 2, BG), jnp.float32),
            pltpu.VMEM((8, 1, BG), jnp.float32),
        ],
        compiler_params=PARAMS,
        cost_estimate=pl.CostEstimate(
            flops=2 * 10**10, bytes_accessed=6 * 10**6, transcendentals=0
        ),
        name="multiply_right",
    )(at, weight_grad, even, odd)


def apply_kernel(
    at_ref, oa_ref, og_ref, mid_ref, own_ref, first_ref, rest_ref, out_ref, sa_ref, sg_ref, a_ref
):
    z, y, c = (at_ref[i] for i in range(3))
    position = 4 * z + 2 * y + c
    owned_a, owned_g = owned_blocks(oa_ref, 8, position), owned_blocks(og_ref, 4, position)

    def place(z_of, y_of, c_of):
        odd = (z ^ z_of) & 1
        turn = (((z ^ odd) - z_of) & 7) >> 1
        return c_of ^ c, 8 * odd + 4 * (y_of ^ y) + turn

    for slot in range(16):
        a_ref[0, slot] = own_ref[GATHERED * slot : GATHERED * (slot + 1)]
        ref, start = (first_ref, slot) if slot < 4 else (rest_ref, slot - 4)
        a_ref[1, slot] = ref[GATHERED * start : GATHERED * (start + 1)]
    for layer in range(LAYERS):
        for quad in range(2):
            results = []
            for k in range(4 * quad, 4 * quad + 4):
                i, slot = place(k, layer % 2, layer // 2)
                left = unpack_wide(a_ref[i, slot, 0:RA].astype(jnp.float32))
                left = left[0:BA, 0:BA].astype(jnp.bfloat16)
                x = mid_ref[layer, BA * k : BA * (k + 1)].astype(jnp.bfloat16)
                results.append(jnp.dot(left, x, preferred_element_type=jnp.float32))
            out_ref[layer, 4 * BA * quad : 4 * BA * (quad + 1)] = jnp.concatenate(
                results, axis=0
            ).astype(jnp.bfloat16)
    stored = []
    for r in range(2):
        block = owned_a[r]
        held = jnp.maximum(block, 0)
        layer = held >> 3
        i, slot = place(held & 7, layer & 1, layer >> 1)
        root = unpack_wide(a_ref[i, slot, 0:RA].astype(jnp.float32))[0:BA, 0:BA]
        stored.append(jnp.where(block >= 0, root, 0.0))
        block = owned_g[r]
        held = jnp.maximum(block, 0)
        layer, k = held >> 2, held & 3
        halves = []
        for half in range(2):
            i, slot = place(layer + 4 * half, k >> 1, k & 1)
            halves.append(a_ref[i, slot, RA - 16 : GATHERED].astype(jnp.float32))
        spare = halves[0][DIAG - RA + 16 : DIAG - RA + 17]
        root = unpack_halves(halves[0][16:48], halves[1][16:48], spare)
        sg_ref[r] = jnp.where(block >= 0, root, 0.0).astype(jnp.bfloat16)
    sa_ref[...] = jnp.stack(stored, axis=1).astype(jnp.bfloat16)


def apply_roots(at, owner_a, owner_g, mid, *gathered):
    whole = pl.BlockSpec(memory_space=pltpu.VMEM)
    return pl.pallas_call(
        apply_kernel,
        in_specs=[pl.BlockSpec(memory_space=pltpu.SMEM)] * 3 + [whole] * 4,
        out_specs=[whole] * 3,
        out_shape=[
            jax.ShapeDtypeStruct(mid.shape, jnp.bfloat16),
            jax.ShapeDtypeStruct((BA, 2, BA), jnp.bfloat16),
            jax.ShapeDtypeStruct((2, BG, BG), jnp.bfloat16),
        ],
        scratch_shapes=[pltpu.VMEM((2, 16, GATHERED, BG), jnp.bfloat16)],
        compiler_params=PARAMS,
        cost_estimate=CHEAP,
        name="apply_roots",
    )(at, owner_a, owner_g, mid, *gathered)


def along_z(shift):
    return [(i, (i + 4 * shift) % 32) for i in range(32)]


OVER_CORE = [(i, i ^ 1) for i in range(32)]
OVER_Y = [(i, i ^ 2) for i in range(32)]
OVER_Z = [(i, i ^ 4) for i in range(32)]
OVER_BOTH = [(i, i ^ 6) for i in range(32)]
AWAY = (4, 6, 3, 1, 2, 0, 5, 7)


def source_of(z, g):
    place = 2 * (((g >> 1) - (z >> 1)) & 3) + ((g ^ z) & 1)
    away = sum(jnp.where(place == i, AWAY[i], 0) for i in range(8))
    return (z + away) & 7


def from_column(odd):
    pairs = []
    for z in range(8):
        for g in range(8):
            away = AWAY[2 * ((g // 2 - z // 2) % 4) + (g + z) % 2]
            source = (z + away) % 8 ^ odd
            pairs += [((source * 4 + r) * 8 + z, (z * 4 + r) * 8 + g) for r in range(4)]
    return sorted(pairs)


def tails_of(messages):
    rows = [x[RA:GATHERED] for x in messages] + [x[DIAG : DIAG + 1] for x in messages]
    return jnp.concatenate(rows + [jnp.zeros((12, BG), jnp.bfloat16)])


def narrow(x):
    return (x * WIRE_SCALE).astype(WIRE)


def widen(x):
    return x.astype(jnp.float32) * (1.0 / WIRE_SCALE)


def shards(hidden_acts, out_grads, weight_grad, owner_a, gradient_block_owner):
    position = lax.axis_index("dp")
    column = lax.axis_index("grp")
    z, y, core = position // 4, lax.rem(position // 2, 2), lax.rem(position, 2)
    scale = 1.0 / (hidden_acts.shape[1] * lax.axis_size("dp"))
    turned = jnp.swapaxes(hidden_acts, 1, 2)

    theirs = covariances(turned, out_grads, 1 - core, z, scale)
    got = lax.ppermute(theirs, "dp", OVER_CORE)
    mine = covariances(turned, out_grads, core, z, scale)

    def chip_sum(of_y):
        one = lax.dynamic_index_in_dim(mine, of_y, 0, False)
        return one + lax.dynamic_index_in_dim(got, of_y, 0, False)

    other, own = chip_sum(1 - y), chip_sum(y)
    got_both = lax.ppermute(narrow(other[1]), "dp", OVER_BOTH)
    got_y = lax.ppermute(narrow(other[0]), "dp", OVER_Y)
    got_z = lax.ppermute(narrow(own[1]), "dp", OVER_Z)
    kept = (own[0] + widen(got_y)) + (widen(got_both) + widen(got_z))

    def message(turn):
        start = (turn // 2) * MSG
        return jnp.concatenate(
            [kept[turn % 2, start : start + RA], kept[turn % 2, RA:MSG]], axis=0
        )

    arrived = [lax.ppermute(narrow(message(t)), "dp", along_z(2 * t)) for t in range(1, 4)]
    total = message(0) + sum(widen(x) for x in arrived)
    packed = inverse_roots(total, z)

    held = [packed] + [lax.ppermute(packed, "dp", along_z(2 * t)) for t in range(1, 4)]
    tails = tails_of(held)
    held = jnp.concatenate(held)
    got_y = lax.ppermute(held, "dp", OVER_Y)
    got_z = lax.ppermute(held, "dp", OVER_Z)
    got_both = lax.ppermute(held, "dp", OVER_BOTH)
    first, tails = lax.optimization_barrier((lax.ppermute(held, "dp", OVER_CORE), tails))
    tails = [lax.ppermute(tails, ("dp", "grp"), pairs) for pairs in map(from_column, (0, 1))]
    gathered = jnp.concatenate([held, got_y, got_z, got_both])
    rest = lax.ppermute(gathered[4 * GATHERED :], "dp", OVER_CORE)

    at = jnp.stack([z, y, core])
    mid = multiply_right(jnp.stack([z, column]), weight_grad, *tails)
    precond_grad, store_a, store_g = apply_roots(
        at, owner_a, gradient_block_owner, mid, gathered, first, rest
    )
    return precond_grad, jnp.swapaxes(store_a, 0, 1)[None, None], store_g[None, None]


def solution(mesh):
    return jax.shard_map(
        shards,
        mesh=mesh,
        in_specs=(
            P(None, "dp", "grp"),
            P(None, "dp", "grp"),
            P(None, "grp", "dp"),
            P(None, "grp"),
            P(None, "grp"),
        ),
        out_specs=(
            P(None, "grp", "dp"),
            P("grp", "dp", None, None, None),
            P("grp", "dp", None, None, None),
        ),
        check_vma=False,
    )
```

```python
import functools

import jax
import jax.numpy as jnp
from jax import lax
from jax.experimental import pallas as pl
from jax.experimental.pallas import tpu as pltpu
from jax.sharding import PartitionSpec as P

ITERS = 12
BA = 172
BG = 128
LAYERS = 4
HALF = 64
NARROW = BA - BG
RA = 144
RG = 64
MSG = RA + RG
PAIR = RA + RG + RA
DIAG = 136
GATHERED = RA + RG // 2
TAIL = 128
TAILS = 144
WIRE = jnp.float16
WIRE_SCALE = 256.0

damping_share = 0.01

SMALL = pltpu.CompilerParams(vmem_limit_bytes=24 << 20)
CHEAP = pl.CostEstimate(flops=10**4, bytes_accessed=10**4, transcendentals=0)
PARAMS = pltpu.CompilerParams(vmem_limit_bytes=48 << 20)


def iota(shape, dim):
    return lax.broadcasted_iota(jnp.int32, shape, dim)


def pack_square(top, bottom):
    row, lane = iota((HALF, BG), 0), iota((HALF, BG), 1)
    turned = pltpu.roll(bottom, HALF, 1)
    folded = jnp.where((lane < HALF) & (row >= lane), turned, top)
    diagonal = jnp.sum(jnp.where(row == lane, top, 0.0), axis=0, keepdims=True)
    return folded, diagonal


def unpack_square(folded, diagonal):
    row, lane = iota((HALF, BG), 0), iota((HALF, BG), 1)
    top = jnp.where(lane > row, folded, jnp.where(lane == row, 0.5 * diagonal, 0.0))
    left = jnp.where(lane < row, folded, jnp.where(lane == row, 0.5 * folded, 0.0))
    bottom = pltpu.roll(left, HALF, 1)
    once = jnp.concatenate([top, bottom], axis=0)
    return once + once.T


def pack_wide(full, spare):
    folded, diagonal = pack_square(full[0:HALF, 0:BG], full[HALF:BG, 0:BG])
    low = full[BG : BG + 48, 0:BG]
    corner = full[BG : BG + 48, BG:256]
    corner = corner[0:24] + pltpu.roll(corner[24:48], HALF, 1)
    both = diagonal + pltpu.roll(spare, HALF, 1)
    last = jnp.where(iota((8, BG), 0) == 0, both, 0.0)
    return folded, low, jnp.concatenate([corner, last], axis=0)


def unpack_wide(packed):
    square = unpack_square(packed[0:HALF], packed[DIAG : DIAG + 1])
    low = packed[HALF : HALF + 48]
    tall = jnp.concatenate([low, jnp.zeros((80, BG), jnp.float32)], axis=0).T
    corner = packed[112:136]
    lane, row = iota((24, BG), 1), iota((24, BG), 0)
    first = jnp.where(lane < NARROW, corner, 0.0)
    second = jnp.where((lane < NARROW) & (row < NARROW - 24), pltpu.roll(corner, HALF, 1), 0.0)
    corner = jnp.concatenate([first, second], axis=0)
    return jnp.concatenate(
        [jnp.concatenate([square, tall], axis=1), jnp.concatenate([low, corner], axis=1)], axis=0
    )


def cov_kernel(scale, at_ref, h_ref, g_ref, o_ref, wide):
    z = at_ref[1]
    spares = []
    for layer in range(LAYERS):
        x = g_ref[layer]
        c = lax.dot_general(x, x, (((0,), (0,)), ((), ())), preferred_element_type=jnp.float32)
        folded, spare = pack_square(c[0:HALF] * scale, c[HALF:BG] * scale)
        spares.append(spare)
        turn = (layer // 2 - (z >> 1)) & 1
        o_ref[0, (layer ^ z) & 1, turn, RA : RA + RG] = folded
    for k in range(8):
        x = h_ref[0, BA * k : BA * (k + 1), :]
        c = lax.dot_general(x, x, (((1,), (1,)), ((), ())), preferred_element_type=jnp.float32)
        wide[k, BG:176] = jnp.zeros((48, 256), jnp.float32)
        wide[k, 0:BA, 0:BA] = c * scale
    for k in range(8):
        turn = (k // 2 - (z >> 1)) & 3
        odd, place = (k ^ z) & 1, turn & 1
        base = pl.multiple_of((turn >> 1) * MSG, 16)
        folded, low, corner = pack_wide(wide.at[k], spares[k % 4])
        o_ref[0, odd, place, pl.ds(base, HALF)] = folded
        o_ref[0, odd, place, pl.ds(base + HALF, 48)] = low
        o_ref[0, odd, place, pl.ds(base + 112, 32)] = corner


def covariances(turned, grads, core, z, scale):
    rows, features = turned.shape[2], turned.shape[1]
    shape = (2, 2, 2, PAIR, BG)
    return pl.pallas_call(
        functools.partial(cov_kernel, scale),
        grid_spec=pltpu.PrefetchScalarGridSpec(
            num_scalar_prefetch=1,
            grid=(2,),
            in_specs=[
                pl.BlockSpec((1, features, rows), lambda i, s: (2 * s[0] + i, 0, 0)),
                pl.BlockSpec((LAYERS, rows, BG), lambda i, s: (0, 0, 2 * i + s[0])),
            ],
            out_specs=pl.BlockSpec((1,) + shape[1:], lambda i, s: (i, 0, 0, 0, 0)),
            scratch_shapes=[pltpu.VMEM((8, 176, 256), jnp.float32)],
        ),
        out_shape=jax.ShapeDtypeStruct(shape, jnp.float32),
        compiler_params=PARAMS,
        cost_estimate=CHEAP,
        name="covariances",
    )(jnp.stack([core, z]), turned, grads)


def parts_of(x):
    high = x.astype(jnp.bfloat16)
    return high, (x - high.astype(jnp.float32)).astype(jnp.bfloat16)


def times(a, b):
    def one(i, j):
        return jnp.dot(a[i], b[j], preferred_element_type=jnp.float32)

    return (one(0, 1) + one(1, 0)) + one(0, 0)


def roots_kernel(z_ref, total_ref, packed_ref, wide, square):
    total = total_ref[...]
    spare = pltpu.roll(total[DIAG : DIAG + 1], HALF, 1)
    blocks = [unpack_wide(total[0:RA])[0:BA, 0:BA], unpack_square(total[RA:MSG], spare)]
    eyes, ys, totals = [], [], []
    for c in blocks:
        width = c.shape[0]
        eye = (iota(c.shape, 0) == iota(c.shape, 1)).astype(jnp.float32)
        damped = c + (damping_share * jnp.sum(c * eye) / width) * eye
        trace = jnp.sum(damped * eye)
        eyes.append(eye)
        ys.append(damped / trace)
        totals.append(trace)
    both = range(2)
    zs = [1.5 * eyes[i] - 0.5 * ys[i] for i in both]
    ys = [times(parts_of(ys[i]), parts_of(zs[i])) for i in both]

    def sweep(_, carry):
        ys, zs = carry
        sy, sz = [parts_of(y) for y in ys], [parts_of(z) for z in zs]
        sp = [parts_of(1.5 * eyes[i] - 0.5 * times(sz[i], sy[i])) for i in both]
        return [times(sy[i], sp[i]) for i in both], [times(sp[i], sz[i]) for i in both]

    ys, zs = lax.fori_loop(0, ITERS - 2, sweep, (ys, zs))
    sz = [parts_of(z) for z in zs]
    sp = [parts_of(1.5 * eyes[i] - 0.5 * times(sz[i], parts_of(ys[i]))) for i in both]
    roots = [times(sp[i], sz[i]) / jnp.sqrt(totals[i]) for i in both]
    wide[...] = jnp.zeros_like(wide)
    wide[0:BA, 0:BA] = roots[0]
    square[...], spare = pack_square(roots[1][0:HALF], roots[1][HALF:BG])
    folded, low, corner = pack_wide(wide, spare)
    packed_ref[0:HALF] = folded.astype(jnp.bfloat16)
    packed_ref[HALF:112] = low.astype(jnp.bfloat16)
    packed_ref[112:RA] = corner.astype(jnp.bfloat16)
    start = pl.multiple_of((z_ref[0] >> 2) * (RG // 2), RG // 2)
    packed_ref[RA:GATHERED] = square[pl.ds(start, RG // 2)].astype(jnp.bfloat16)


def inverse_roots(total, z):
    whole = pl.BlockSpec(memory_space=pltpu.VMEM)
    return pl.pallas_call(
        roots_kernel,
        in_specs=[pl.BlockSpec(memory_space=pltpu.SMEM), whole],
        out_specs=whole,
        out_shape=jax.ShapeDtypeStruct((GATHERED, BG), jnp.bfloat16),
        scratch_shapes=[pltpu.VMEM((176, 256), jnp.float32), pltpu.VMEM((RG, BG), jnp.float32)],
        compiler_params=PARAMS,
        cost_estimate=CHEAP,
        name="inverse_roots",
    )(z.reshape(1), total)


def unpack_halves(first, second, spare):
    return unpack_square(jnp.concatenate([first, second], axis=0), pltpu.roll(spare, HALF, 1))


def owned_blocks(owners_ref, per_layer, position):
    first = second = jnp.int32(-1)
    for place in range(LAYERS * per_layer):
        mine = owners_ref[place // per_layer, place % per_layer] == position
        second = jnp.where(mine & (first >= 0), place, second)
        first = jnp.where(mine & (first < 0), place, first)
    return first, second


def right_kernel(at_ref, w_ref, even_ref, odd_ref, mid_ref, right, spares):
    start = source_of(at_ref[0], at_ref[1])
    for odd, ref in enumerate((even_ref, odd_ref)):
        for turn in range(4):
            source = ((start ^ odd) - 2 * turn) & 7
            right[source] = ref[32 * turn : 32 * (turn + 1)].astype(jnp.float32)
            spares[source] = ref[128:144].astype(jnp.float32)[turn : turn + 1]
    for layer in range(LAYERS):
        root = unpack_halves(right[layer], right[layer + 4], spares[layer]).astype(jnp.bfloat16)
        product = jnp.dot(w_ref[layer], root, preferred_element_type=jnp.float32)
        mid_ref[layer] = product.astype(jnp.bfloat16).astype(jnp.float32)


def multiply_right(at, weight_grad, even, odd):
    whole = pl.BlockSpec(memory_space=pltpu.VMEM)
    return pl.pallas_call(
        right_kernel,
        in_specs=[pl.BlockSpec(memory_space=pltpu.SMEM)] + [whole] * 3,
        out_specs=whole,
        out_shape=jax.ShapeDtypeStruct(weight_grad.shape, jnp.float32),
        scratch_shapes=[
            pltpu.VMEM((8, RG // 2, BG), jnp.float32),
            pltpu.VMEM((8, 1, BG), jnp.float32),
        ],
        compiler_params=SMALL,
        cost_estimate=pl.CostEstimate(
            flops=2 * 10**10, bytes_accessed=6 * 10**6, transcendentals=0
        ),
        name="multiply_right",
    )(at, weight_grad, even, odd)


def unpack_kernel(*refs):
    full_ref, tails_ref = refs[-2:]
    slot = 0
    for ref in refs[:-2]:
        for start in range(0, ref.shape[0], GATHERED):
            packed = ref[start : start + RA].astype(jnp.float32)
            full_ref[slot] = unpack_wide(packed).astype(jnp.bfloat16)
            tails_ref[slot] = ref[start + TAIL : start + GATHERED]
            slot += 1


def unpack_roots(*messages):
    whole = pl.BlockSpec(memory_space=pltpu.VMEM)
    return pl.pallas_call(
        unpack_kernel,
        in_specs=[whole] * len(messages),
        out_specs=[whole] * 2,
        out_shape=[
            jax.ShapeDtypeStruct((16, 176, 256), jnp.bfloat16),
            jax.ShapeDtypeStruct((16, GATHERED - TAIL, BG), jnp.bfloat16),
        ],
        compiler_params=SMALL,
        cost_estimate=CHEAP,
        name="unpack_roots",
    )(*messages)


def apply_kernel(
    at_ref, oa_ref, og_ref, mid_ref, full0_ref, full1_ref, tails0_ref, tails1_ref,
    out_ref, sa_ref, sg_ref,
):
    z, y, c = (at_ref[i] for i in range(3))
    position = 4 * z + 2 * y + c
    owned_a, owned_g = owned_blocks(oa_ref, 8, position), owned_blocks(og_ref, 4, position)

    def place(z_of, y_of, c_of):
        odd = (z ^ z_of) & 1
        turn = (((z ^ odd) - z_of) & 7) >> 1
        return c_of ^ c, 8 * odd + 4 * (y_of ^ y) + turn

    for beside, full_ref in enumerate((full0_ref, full1_ref)):
        for odd in range(2):
            layer = 2 * (c ^ beside) + odd
            for quad in range(2):
                results = []
                for k in range(4 * quad, 4 * quad + 4):
                    _, slot = place(k, odd, c ^ beside)
                    left = full_ref[slot, 0:BA, 0:BA]
                    x = mid_ref[layer, BA * k : BA * (k + 1)].astype(jnp.bfloat16)
                    results.append(jnp.dot(left, x, preferred_element_type=jnp.float32))
                out_ref[layer, 4 * BA * quad : 4 * BA * (quad + 1)] = jnp.concatenate(
                    results, axis=0
                ).astype(jnp.bfloat16)

    def chosen(beside, slot, own_ref, other_ref):
        own, other = own_ref[slot].astype(jnp.float32), other_ref[slot].astype(jnp.float32)
        return jnp.where(beside == 0, own, other)

    stored = []
    for r in range(2):
        block = owned_a[r]
        held = jnp.maximum(block, 0)
        layer = held >> 3
        i, slot = place(held & 7, layer & 1, layer >> 1)
        root = chosen(i, slot, full0_ref, full1_ref)[0:BA, 0:BA]
        stored.append(jnp.where(block >= 0, root, 0.0))
        block = owned_g[r]
        held = jnp.maximum(block, 0)
        layer, k = held >> 2, held & 3
        halves = []
        for half in range(2):
            i, slot = place(layer + 4 * half, k >> 1, k & 1)
            halves.append(chosen(i, slot, tails0_ref, tails1_ref))
        spare = halves[0][DIAG - TAIL : DIAG - TAIL + 1]
        root = unpack_halves(halves[0][16:48], halves[1][16:48], spare)
        sg_ref[r] = jnp.where(block >= 0, root, 0.0).astype(jnp.bfloat16)
    sa_ref[...] = jnp.stack(stored, axis=1).astype(jnp.bfloat16)


def apply_roots(at, owner_a, owner_g, mid, *gathered):
    whole = pl.BlockSpec(memory_space=pltpu.VMEM)
    return pl.pallas_call(
        apply_kernel,
        in_specs=[pl.BlockSpec(memory_space=pltpu.SMEM)] * 3 + [whole] * 5,
        out_specs=[whole] * 3,
        out_shape=[
            jax.ShapeDtypeStruct(mid.shape, jnp.bfloat16),
            jax.ShapeDtypeStruct((BA, 2, BA), jnp.bfloat16),
            jax.ShapeDtypeStruct((2, BG, BG), jnp.bfloat16),
        ],
        compiler_params=SMALL,
        cost_estimate=CHEAP,
        name="apply_roots",
    )(at, owner_a, owner_g, mid, *gathered)


def along_z(shift):
    return [(i, (i + 4 * shift) % 32) for i in range(32)]


OVER_CORE = [(i, i ^ 1) for i in range(32)]
OVER_Y = [(i, i ^ 2) for i in range(32)]
OVER_Z = [(i, i ^ 4) for i in range(32)]
OVER_BOTH = [(i, i ^ 6) for i in range(32)]
AWAY = (4, 6, 3, 1, 2, 0, 5, 7)


def source_of(z, g):
    place = 2 * (((g >> 1) - (z >> 1)) & 3) + ((g ^ z) & 1)
    away = sum(jnp.where(place == i, AWAY[i], 0) for i in range(8))
    return (z + away) & 7


def from_column(odd):
    pairs = []
    for z in range(8):
        for g in range(8):
            away = AWAY[2 * ((g // 2 - z // 2) % 4) + (g + z) % 2]
            source = (z + away) % 8 ^ odd
            pairs += [((source * 4 + r) * 8 + z, (z * 4 + r) * 8 + g) for r in range(4)]
    return sorted(pairs)


def tails_of(messages):
    rows = [x[RA:GATHERED] for x in messages] + [x[DIAG : DIAG + 1] for x in messages]
    return jnp.concatenate(rows + [jnp.zeros((12, BG), jnp.bfloat16)])


def narrow(x):
    return (x * WIRE_SCALE).astype(WIRE)


def widen(x):
    return x.astype(jnp.float32) * (1.0 / WIRE_SCALE)


def shards(hidden_acts, out_grads, weight_grad, owner_a, gradient_block_owner):
    position = lax.axis_index("dp")
    column = lax.axis_index("grp")
    z, y, core = position // 4, lax.rem(position // 2, 2), lax.rem(position, 2)
    scale = 1.0 / (hidden_acts.shape[1] * lax.axis_size("dp"))
    turned = jnp.swapaxes(hidden_acts, 1, 2)

    theirs = covariances(turned, out_grads, 1 - core, z, scale)
    got = lax.ppermute(theirs, "dp", OVER_CORE)
    mine = covariances(turned, out_grads, core, z, scale)

    def chip_sum(of_y):
        one = lax.dynamic_index_in_dim(mine, of_y, 0, False)
        return one + lax.dynamic_index_in_dim(got, of_y, 0, False)

    other, own = chip_sum(1 - y), chip_sum(y)
    got_both = lax.ppermute(narrow(other[1]), "dp", OVER_BOTH)
    got_y = lax.ppermute(narrow(other[0]), "dp", OVER_Y)
    got_z = lax.ppermute(narrow(own[1]), "dp", OVER_Z)
    kept = (own[0] + widen(got_y)) + (widen(got_both) + widen(got_z))

    def message(turn):
        start = (turn // 2) * MSG
        return jnp.concatenate(
            [kept[turn % 2, start : start + RA], kept[turn % 2, RA:MSG]], axis=0
        )

    arrived = [lax.ppermute(narrow(message(t)), "dp", along_z(2 * t)) for t in range(1, 4)]
    total = message(0) + sum(widen(x) for x in arrived)
    packed = inverse_roots(total, z)

    held = [packed] + [lax.ppermute(packed, "dp", along_z(2 * t)) for t in range(1, 4)]
    tails = tails_of(held)
    held = jnp.concatenate(held)
    got_y = lax.ppermute(held, "dp", OVER_Y)
    got_z = lax.ppermute(held, "dp", OVER_Z)
    got_both = lax.ppermute(held, "dp", OVER_BOTH)
    first, tails = lax.optimization_barrier((lax.ppermute(held, "dp", OVER_CORE), tails))
    tails = [lax.ppermute(tails, ("dp", "grp"), pairs) for pairs in map(from_column, (0, 1))]
    gathered = jnp.concatenate([held, got_y, got_z, got_both])
    rest = lax.ppermute(gathered[4 * GATHERED :], "dp", OVER_CORE)

    at = jnp.stack([z, y, core])
    full_own, tails_own = unpack_roots(gathered)
    full_beside, tails_beside = unpack_roots(first, rest)
    mid = multiply_right(jnp.stack([z, column]), weight_grad, *tails)
    precond_grad, store_a, store_g = apply_roots(
        at, owner_a, gradient_block_owner, mid, full_own, full_beside, tails_own, tails_beside
    )
    return precond_grad, jnp.swapaxes(store_a, 0, 1)[None, None], store_g[None, None]


def solution(mesh):
    return jax.shard_map(
        shards,
        mesh=mesh,
        in_specs=(
            P(None, "dp", "grp"),
            P(None, "dp", "grp"),
            P(None, "grp", "dp"),
            P(None, "grp"),
            P(None, "grp"),
        ),
        out_specs=(
            P(None, "grp", "dp"),
            P("grp", "dp", None, None, None),
            P("grp", "dp", None, None, None),
        ),
        check_vma=False,
    )
```

```python
import functools

import jax
import jax.numpy as jnp
from jax import lax
from jax.experimental import pallas as pl
from jax.experimental.pallas import tpu as pltpu
from jax.sharding import PartitionSpec as P

ITERS = 12
BA = 172
BG = 128
LAYERS = 4
HALF = 64
NARROW = BA - BG
RA = 144
RG = 64
MSG = RA + RG
PAIR = RA + RG + RA
DIAG = 136
GATHERED = RA + RG // 2
TAIL = 128
TAILS = 144
WIRE = jnp.float16
WIRE_SCALE = 256.0

damping_share = 0.01

SMALL = pltpu.CompilerParams(vmem_limit_bytes=24 << 20)
CHEAP = pl.CostEstimate(flops=10**4, bytes_accessed=10**4, transcendentals=0)
PARAMS = pltpu.CompilerParams(vmem_limit_bytes=48 << 20)


def iota(shape, dim):
    return lax.broadcasted_iota(jnp.int32, shape, dim)


def pack_square(top, bottom):
    row, lane = iota((HALF, BG), 0), iota((HALF, BG), 1)
    turned = pltpu.roll(bottom, HALF, 1)
    folded = jnp.where((lane < HALF) & (row >= lane), turned, top)
    diagonal = jnp.sum(jnp.where(row == lane, top, 0.0), axis=0, keepdims=True)
    return folded, diagonal


def unpack_square(folded, diagonal):
    row, lane = iota((HALF, BG), 0), iota((HALF, BG), 1)
    top = jnp.where(lane > row, folded, jnp.where(lane == row, 0.5 * diagonal, 0.0))
    left = jnp.where(lane < row, folded, jnp.where(lane == row, 0.5 * folded, 0.0))
    bottom = pltpu.roll(left, HALF, 1)
    once = jnp.concatenate([top, bottom], axis=0)
    return once + once.T


def pack_wide(full, spare):
    folded, diagonal = pack_square(full[0:HALF, 0:BG], full[HALF:BG, 0:BG])
    low = full[BG : BG + 48, 0:BG]
    corner = full[BG : BG + 48, BG:256]
    corner = corner[0:24] + pltpu.roll(corner[24:48], HALF, 1)
    both = diagonal + pltpu.roll(spare, HALF, 1)
    last = jnp.where(iota((8, BG), 0) == 0, both, 0.0)
    return folded, low, jnp.concatenate([corner, last], axis=0)


def unpack_wide(packed):
    square = unpack_square(packed[0:HALF], packed[DIAG : DIAG + 1])
    low = packed[HALF : HALF + 48]
    tall = jnp.concatenate([low, jnp.zeros((80, BG), jnp.float32)], axis=0).T
    corner = packed[112:136]
    lane, row = iota((24, BG), 1), iota((24, BG), 0)
    first = jnp.where(lane < NARROW, corner, 0.0)
    second = jnp.where((lane < NARROW) & (row < NARROW - 24), pltpu.roll(corner, HALF, 1), 0.0)
    corner = jnp.concatenate([first, second], axis=0)
    return jnp.concatenate(
        [jnp.concatenate([square, tall], axis=1), jnp.concatenate([low, corner], axis=1)], axis=0
    )


def cov_kernel(scale, at_ref, h_ref, g_ref, o_ref, wide):
    z = at_ref[1]
    spares = []
    for layer in range(LAYERS):
        x = g_ref[layer]
        c = lax.dot_general(x, x, (((0,), (0,)), ((), ())), preferred_element_type=jnp.float32)
        folded, spare = pack_square(c[0:HALF] * scale, c[HALF:BG] * scale)
        spares.append(spare)
        turn = (layer // 2 - (z >> 1)) & 1
        o_ref[0, (layer ^ z) & 1, turn, RA : RA + RG] = folded
    for k in range(8):
        x = h_ref[0, BA * k : BA * (k + 1), :]
        c = lax.dot_general(x, x, (((1,), (1,)), ((), ())), preferred_element_type=jnp.float32)
        wide[k, BG:176] = jnp.zeros((48, 256), jnp.float32)
        wide[k, 0:BA, 0:BA] = c * scale
    for k in range(8):
        turn = (k // 2 - (z >> 1)) & 3
        odd, place = (k ^ z) & 1, turn & 1
        base = pl.multiple_of((turn >> 1) * MSG, 16)
        folded, low, corner = pack_wide(wide.at[k], spares[k % 4])
        o_ref[0, odd, place, pl.ds(base, HALF)] = folded
        o_ref[0, odd, place, pl.ds(base + HALF, 48)] = low
        o_ref[0, odd, place, pl.ds(base + 112, 32)] = corner


def covariances(turned, grads, core, z, scale):
    rows, features = turned.shape[2], turned.shape[1]
    shape = (2, 2, 2, PAIR, BG)
    return pl.pallas_call(
        functools.partial(cov_kernel, scale),
        grid_spec=pltpu.PrefetchScalarGridSpec(
            num_scalar_prefetch=1,
            grid=(2,),
            in_specs=[
                pl.BlockSpec((1, features, rows), lambda i, s: (2 * s[0] + i, 0, 0)),
                pl.BlockSpec((LAYERS, rows, BG), lambda i, s: (0, 0, 2 * i + s[0])),
            ],
            out_specs=pl.BlockSpec((1,) + shape[1:], lambda i, s: (i, 0, 0, 0, 0)),
            scratch_shapes=[pltpu.VMEM((8, 176, 256), jnp.float32)],
        ),
        out_shape=jax.ShapeDtypeStruct(shape, jnp.float32),
        compiler_params=PARAMS,
        cost_estimate=CHEAP,
        name="covariances",
    )(jnp.stack([core, z]), turned, grads)


def parts_of(x):
    high = x.astype(jnp.bfloat16)
    return high, (x - high.astype(jnp.float32)).astype(jnp.bfloat16)


def times(a, b):
    def one(i, j):
        return jnp.dot(a[i], b[j], preferred_element_type=jnp.float32)

    return (one(0, 1) + one(1, 0)) + one(0, 0)


def roots_kernel(z_ref, total_ref, packed_ref, wide, square):
    total = total_ref[...]
    spare = pltpu.roll(total[DIAG : DIAG + 1], HALF, 1)
    blocks = [unpack_wide(total[0:RA])[0:BA, 0:BA], unpack_square(total[RA:MSG], spare)]
    eyes, ys, totals = [], [], []
    for c in blocks:
        width = c.shape[0]
        eye = (iota(c.shape, 0) == iota(c.shape, 1)).astype(jnp.float32)
        damped = c + (damping_share * jnp.sum(c * eye) / width) * eye
        trace = jnp.sum(damped * eye)
        eyes.append(eye)
        ys.append(damped / trace)
        totals.append(trace)
    both = range(2)
    zs = [1.5 * eyes[i] - 0.5 * ys[i] for i in both]
    ys = [times(parts_of(ys[i]), parts_of(zs[i])) for i in both]

    def sweep(_, carry):
        ys, zs = carry
        sy, sz = [parts_of(y) for y in ys], [parts_of(z) for z in zs]
        sp = [parts_of(1.5 * eyes[i] - 0.5 * times(sz[i], sy[i])) for i in both]
        return [times(sy[i], sp[i]) for i in both], [times(sp[i], sz[i]) for i in both]

    ys, zs = lax.fori_loop(0, ITERS - 2, sweep, (ys, zs))
    sz = [parts_of(z) for z in zs]
    sp = [parts_of(1.5 * eyes[i] - 0.5 * times(sz[i], parts_of(ys[i]))) for i in both]
    roots = [times(sp[i], sz[i]) / jnp.sqrt(totals[i]) for i in both]
    wide[...] = jnp.zeros_like(wide)
    wide[0:BA, 0:BA] = roots[0]
    square[...], spare = pack_square(roots[1][0:HALF], roots[1][HALF:BG])
    folded, low, corner = pack_wide(wide, spare)
    packed_ref[0:HALF] = folded.astype(jnp.bfloat16)
    packed_ref[HALF:112] = low.astype(jnp.bfloat16)
    packed_ref[112:RA] = corner.astype(jnp.bfloat16)
    start = pl.multiple_of((z_ref[0] >> 2) * (RG // 2), RG // 2)
    packed_ref[RA:GATHERED] = square[pl.ds(start, RG // 2)].astype(jnp.bfloat16)


def inverse_roots(total, z):
    whole = pl.BlockSpec(memory_space=pltpu.VMEM)
    return pl.pallas_call(
        roots_kernel,
        in_specs=[pl.BlockSpec(memory_space=pltpu.SMEM), whole],
        out_specs=whole,
        out_shape=jax.ShapeDtypeStruct((GATHERED, BG), jnp.bfloat16),
        scratch_shapes=[pltpu.VMEM((176, 256), jnp.float32), pltpu.VMEM((RG, BG), jnp.float32)],
        compiler_params=PARAMS,
        cost_estimate=CHEAP,
        name="inverse_roots",
    )(z.reshape(1), total)


def unpack_halves(first, second, spare):
    return unpack_square(jnp.concatenate([first, second], axis=0), pltpu.roll(spare, HALF, 1))


def owned_blocks(owners_ref, per_layer, position):
    first = second = jnp.int32(-1)
    for place in range(LAYERS * per_layer):
        mine = owners_ref[place // per_layer, place % per_layer] == position
        second = jnp.where(mine & (first >= 0), place, second)
        first = jnp.where(mine & (first < 0), place, first)
    return first, second


def right_kernel(at_ref, w_ref, even_ref, odd_ref, mid_ref, right, spares):
    start = source_of(at_ref[0], at_ref[1])
    for odd, ref in enumerate((even_ref, odd_ref)):
        for turn in range(4):
            source = ((start ^ odd) - 2 * turn) & 7
            right[source] = ref[32 * turn : 32 * (turn + 1)].astype(jnp.float32)
            spares[source] = ref[128:144].astype(jnp.float32)[turn : turn + 1]
    for layer in range(LAYERS):
        root = unpack_halves(right[layer], right[layer + 4], spares[layer]).astype(jnp.bfloat16)
        product = jnp.dot(w_ref[layer], root, preferred_element_type=jnp.float32)
        mid_ref[layer] = product.astype(jnp.bfloat16).astype(jnp.float32)


def multiply_right(at, weight_grad, even, odd):
    whole = pl.BlockSpec(memory_space=pltpu.VMEM)
    return pl.pallas_call(
        right_kernel,
        in_specs=[pl.BlockSpec(memory_space=pltpu.SMEM)] + [whole] * 3,
        out_specs=whole,
        out_shape=jax.ShapeDtypeStruct(weight_grad.shape, jnp.float32),
        scratch_shapes=[
            pltpu.VMEM((8, RG // 2, BG), jnp.float32),
            pltpu.VMEM((8, 1, BG), jnp.float32),
        ],
        compiler_params=SMALL,
        cost_estimate=pl.CostEstimate(
            flops=2 * 10**10, bytes_accessed=6 * 10**6, transcendentals=0
        ),
        name="multiply_right",
    )(at, weight_grad, even, odd)


def unpack_kernel(*refs):
    full_ref, tails_ref = refs[-2:]
    slot = 0
    for ref in refs[:-2]:
        for start in range(0, ref.shape[0], GATHERED):
            packed = ref[start : start + RA].astype(jnp.float32)
            full_ref[slot] = unpack_wide(packed).astype(jnp.bfloat16)
            tails_ref[slot] = ref[start + TAIL : start + GATHERED]
            slot += 1


def unpack_roots(*messages):
    whole = pl.BlockSpec(memory_space=pltpu.VMEM)
    return pl.pallas_call(
        unpack_kernel,
        in_specs=[whole] * len(messages),
        out_specs=[whole] * 2,
        out_shape=[
            jax.ShapeDtypeStruct((16, 176, 256), jnp.bfloat16),
            jax.ShapeDtypeStruct((16, GATHERED - TAIL, BG), jnp.bfloat16),
        ],
        compiler_params=SMALL,
        cost_estimate=CHEAP,
        name="unpack_roots",
    )(*messages)


def apply_kernel(
    at_ref, oa_ref, og_ref, mid_ref, full0_ref, full1_ref, tails0_ref, tails1_ref,
    out_ref, sa_ref, sg_ref,
):
    z, y, c = (at_ref[i] for i in range(3))

    def place(z_of, y_of, c_of):
        odd = (z ^ z_of) & 1
        turn = (((z ^ odd) - z_of) & 7) >> 1
        return c_of ^ c, 8 * odd + 4 * (y_of ^ y) + turn

    step = pl.program_id(0)
    odd = step & 1

    def multiply(beside, full_ref):
        layer = 2 * (c ^ beside) + odd
        for quad in range(2):
            results = []
            for k in range(4 * quad, 4 * quad + 4):
                _, slot = place(k, odd, c ^ beside)
                left = full_ref[slot, 0:BA, 0:BA]
                x = mid_ref[layer, BA * k : BA * (k + 1)].astype(jnp.bfloat16)
                results.append(jnp.dot(left, x, preferred_element_type=jnp.float32))
            out_ref[0, 4 * BA * quad : 4 * BA * (quad + 1)] = jnp.concatenate(
                results, axis=0
            ).astype(jnp.bfloat16)

    @pl.when(step < 2)
    def _():
        multiply(0, full0_ref)

    @pl.when(step >= 2)
    def _():
        multiply(1, full1_ref)

    def chosen(beside, slot, own_ref, other_ref):
        own, other = own_ref[slot].astype(jnp.float32), other_ref[slot].astype(jnp.float32)
        return jnp.where(beside == 0, own, other)

    @pl.when(step == 0)
    def _():
        position = 4 * z + 2 * y + c
        owned_a, owned_g = owned_blocks(oa_ref, 8, position), owned_blocks(og_ref, 4, position)
        stored = []
        for r in range(2):
            block = owned_a[r]
            held = jnp.maximum(block, 0)
            layer = held >> 3
            i, slot = place(held & 7, layer & 1, layer >> 1)
            root = chosen(i, slot, full0_ref, full1_ref)[0:BA, 0:BA]
            stored.append(jnp.where(block >= 0, root, 0.0))
            block = owned_g[r]
            held = jnp.maximum(block, 0)
            layer, k = held >> 2, held & 3
            halves = []
            for half in range(2):
                i, slot = place(layer + 4 * half, k >> 1, k & 1)
                halves.append(chosen(i, slot, tails0_ref, tails1_ref))
            spare = halves[0][DIAG - TAIL : DIAG - TAIL + 1]
            root = unpack_halves(halves[0][16:48], halves[1][16:48], spare)
            sg_ref[r] = jnp.where(block >= 0, root, 0.0).astype(jnp.bfloat16)
        sa_ref[...] = jnp.stack(stored, axis=1).astype(jnp.bfloat16)


def apply_roots(at, owner_a, owner_g, mid, *gathered):
    whole = pl.BlockSpec(memory_space=pltpu.VMEM)
    scalars = pl.BlockSpec(memory_space=pltpu.SMEM)
    layer_block = (1,) + mid.shape[1:]
    return pl.pallas_call(
        apply_kernel,
        grid_spec=pltpu.PrefetchScalarGridSpec(
            num_scalar_prefetch=1,
            grid=(LAYERS,),
            in_specs=[scalars] * 2 + [whole] * 5,
            out_specs=[
                pl.BlockSpec(layer_block, lambda i, s: (2 * (s[2] ^ (i >> 1)) + (i & 1), 0, 0)),
                pl.BlockSpec((BA, 2, BA), lambda i, s: (0, 0, 0)),
                pl.BlockSpec((2, BG, BG), lambda i, s: (0, 0, 0)),
            ],
        ),
        out_shape=[
            jax.ShapeDtypeStruct(mid.shape, jnp.bfloat16),
            jax.ShapeDtypeStruct((BA, 2, BA), jnp.bfloat16),
            jax.ShapeDtypeStruct((2, BG, BG), jnp.bfloat16),
        ],
        compiler_params=SMALL,
        cost_estimate=CHEAP,
        name="apply_roots",
    )(at, owner_a, owner_g, mid, *gathered)


def along_z(shift):
    return [(i, (i + 4 * shift) % 32) for i in range(32)]


OVER_CORE = [(i, i ^ 1) for i in range(32)]
OVER_Y = [(i, i ^ 2) for i in range(32)]
OVER_Z = [(i, i ^ 4) for i in range(32)]
OVER_BOTH = [(i, i ^ 6) for i in range(32)]
AWAY = (4, 6, 3, 1, 2, 0, 5, 7)


def source_of(z, g):
    place = 2 * (((g >> 1) - (z >> 1)) & 3) + ((g ^ z) & 1)
    away = sum(jnp.where(place == i, AWAY[i], 0) for i in range(8))
    return (z + away) & 7


def from_column(odd):
    pairs = []
    for z in range(8):
        for g in range(8):
            away = AWAY[2 * ((g // 2 - z // 2) % 4) + (g + z) % 2]
            source = (z + away) % 8 ^ odd
            pairs += [((source * 4 + r) * 8 + z, (z * 4 + r) * 8 + g) for r in range(4)]
    return sorted(pairs)


def tails_of(messages):
    rows = [x[RA:GATHERED] for x in messages] + [x[DIAG : DIAG + 1] for x in messages]
    return jnp.concatenate(rows + [jnp.zeros((12, BG), jnp.bfloat16)])


def narrow(x):
    return (x * WIRE_SCALE).astype(WIRE)


def widen(x):
    return x.astype(jnp.float32) * (1.0 / WIRE_SCALE)


def shards(hidden_acts, out_grads, weight_grad, owner_a, gradient_block_owner):
    position = lax.axis_index("dp")
    column = lax.axis_index("grp")
    z, y, core = position // 4, lax.rem(position // 2, 2), lax.rem(position, 2)
    scale = 1.0 / (hidden_acts.shape[1] * lax.axis_size("dp"))
    turned = jnp.swapaxes(hidden_acts, 1, 2)

    theirs = covariances(turned, out_grads, 1 - core, z, scale)
    got = lax.ppermute(theirs, "dp", OVER_CORE)
    mine = covariances(turned, out_grads, core, z, scale)

    def chip_sum(of_y):
        one = lax.dynamic_index_in_dim(mine, of_y, 0, False)
        return one + lax.dynamic_index_in_dim(got, of_y, 0, False)

    other, own = chip_sum(1 - y), chip_sum(y)
    got_both = lax.ppermute(narrow(other[1]), "dp", OVER_BOTH)
    got_y = lax.ppermute(narrow(other[0]), "dp", OVER_Y)
    got_z = lax.ppermute(narrow(own[1]), "dp", OVER_Z)
    kept = (own[0] + widen(got_y)) + (widen(got_both) + widen(got_z))

    def message(turn):
        start = (turn // 2) * MSG
        return jnp.concatenate(
            [kept[turn % 2, start : start + RA], kept[turn % 2, RA:MSG]], axis=0
        )

    arrived = [lax.ppermute(narrow(message(t)), "dp", along_z(2 * t)) for t in range(1, 4)]
    total = message(0) + sum(widen(x) for x in arrived)
    packed = inverse_roots(total, z)

    held = [packed] + [lax.ppermute(packed, "dp", along_z(2 * t)) for t in range(1, 4)]
    tails = tails_of(held)
    held = jnp.concatenate(held)
    got_y = lax.ppermute(held, "dp", OVER_Y)
    got_z = lax.ppermute(held, "dp", OVER_Z)
    got_both = lax.ppermute(held, "dp", OVER_BOTH)
    first, tails = lax.optimization_barrier((lax.ppermute(held, "dp", OVER_CORE), tails))
    tails = [lax.ppermute(tails, ("dp", "grp"), pairs) for pairs in map(from_column, (0, 1))]
    gathered = jnp.concatenate([held, got_y, got_z, got_both])
    rest = lax.ppermute(gathered[4 * GATHERED :], "dp", OVER_CORE)

    at = jnp.stack([z, y, core])
    full_own, tails_own = unpack_roots(gathered)
    full_beside, tails_beside = unpack_roots(first, rest)
    mid = multiply_right(jnp.stack([z, column]), weight_grad, *tails)
    precond_grad, store_a, store_g = apply_roots(
        at, owner_a, gradient_block_owner, mid, full_own, full_beside, tails_own, tails_beside
    )
    return precond_grad, jnp.swapaxes(store_a, 0, 1)[None, None], store_g[None, None]


def solution(mesh):
    return jax.shard_map(
        shards,
        mesh=mesh,
        in_specs=(
            P(None, "dp", "grp"),
            P(None, "dp", "grp"),
            P(None, "grp", "dp"),
            P(None, "grp"),
            P(None, "grp"),
        ),
        out_specs=(
            P(None, "grp", "dp"),
            P("grp", "dp", None, None, None),
            P("grp", "dp", None, None, None),
        ),
        check_vma=False,
    )
```

```python
import functools

import jax
import jax.numpy as jnp
from jax import lax
from jax.experimental import pallas as pl
from jax.experimental.pallas import tpu as pltpu
from jax.sharding import PartitionSpec as P

ITERS = 12
BA = 172
BG = 128
LAYERS = 4
HALF = 64
NARROW = BA - BG
RA = 144
RG = 64
MSG = RA + RG
PAIR = RA + RG + RA
DIAG = 136
GATHERED = RA + RG // 2
TAILS = 144
WIRE = jnp.float16
WIRE_SCALE = 256.0

damping_share = 0.01

CHEAP = pl.CostEstimate(flops=10**4, bytes_accessed=10**4, transcendentals=0)
PARAMS = pltpu.CompilerParams(vmem_limit_bytes=48 << 20)


def iota(shape, dim):
    return lax.broadcasted_iota(jnp.int32, shape, dim)


def pack_square(top, bottom):
    row, lane = iota((HALF, BG), 0), iota((HALF, BG), 1)
    turned = pltpu.roll(bottom, HALF, 1)
    folded = jnp.where((lane < HALF) & (row >= lane), turned, top)
    diagonal = jnp.sum(jnp.where(row == lane, top, 0.0), axis=0, keepdims=True)
    return folded, diagonal


def unpack_square(folded, diagonal):
    row, lane = iota((HALF, BG), 0), iota((HALF, BG), 1)
    top = jnp.where(lane > row, folded, jnp.where(lane == row, 0.5 * diagonal, 0.0))
    left = jnp.where(lane < row, folded, jnp.where(lane == row, 0.5 * folded, 0.0))
    bottom = pltpu.roll(left, HALF, 1)
    once = jnp.concatenate([top, bottom], axis=0)
    return once + once.T


def pack_wide(full, spare):
    folded, diagonal = pack_square(full[0:HALF, 0:BG], full[HALF:BG, 0:BG])
    low = full[BG : BG + 48, 0:BG]
    corner = full[BG : BG + 48, BG:256]
    corner = corner[0:24] + pltpu.roll(corner[24:48], HALF, 1)
    both = diagonal + pltpu.roll(spare, HALF, 1)
    last = jnp.where(iota((8, BG), 0) == 0, both, 0.0)
    return folded, low, jnp.concatenate([corner, last], axis=0)


def unpack_wide(packed):
    square = unpack_square(packed[0:HALF], packed[DIAG : DIAG + 1])
    low = packed[HALF : HALF + 48]
    tall = jnp.concatenate([low, jnp.zeros((80, BG), jnp.float32)], axis=0).T
    corner = packed[112:136]
    lane, row = iota((24, BG), 1), iota((24, BG), 0)
    first = jnp.where(lane < NARROW, corner, 0.0)
    second = jnp.where((lane < NARROW) & (row < NARROW - 24), pltpu.roll(corner, HALF, 1), 0.0)
    corner = jnp.concatenate([first, second], axis=0)
    return jnp.concatenate(
        [jnp.concatenate([square, tall], axis=1), jnp.concatenate([low, corner], axis=1)], axis=0
    )


def cov_kernel(scale, at_ref, h_ref, g_ref, o_ref, wide):
    z = at_ref[1]
    spares = []
    for layer in range(LAYERS):
        x = g_ref[layer]
        c = lax.dot_general(x, x, (((0,), (0,)), ((), ())), preferred_element_type=jnp.float32)
        folded, spare = pack_square(c[0:HALF] * scale, c[HALF:BG] * scale)
        spares.append(spare)
        turn = (layer // 2 - (z >> 1)) & 1
        o_ref[0, (layer ^ z) & 1, turn, RA : RA + RG] = folded
    for k in range(8):
        x = h_ref[0, BA * k : BA * (k + 1), :]
        c = lax.dot_general(x, x, (((1,), (1,)), ((), ())), preferred_element_type=jnp.float32)
        wide[k, BG:176] = jnp.zeros((48, 256), jnp.float32)
        wide[k, 0:BA, 0:BA] = c * scale
    for k in range(8):
        turn = (k // 2 - (z >> 1)) & 3
        odd, place = (k ^ z) & 1, turn & 1
        base = pl.multiple_of((turn >> 1) * MSG, 16)
        folded, low, corner = pack_wide(wide.at[k], spares[k % 4])
        o_ref[0, odd, place, pl.ds(base, HALF)] = folded
        o_ref[0, odd, place, pl.ds(base + HALF, 48)] = low
        o_ref[0, odd, place, pl.ds(base + 112, 32)] = corner


def covariances(turned, grads, core, z, scale):
    rows, features = turned.shape[2], turned.shape[1]
    shape = (2, 2, 2, PAIR, BG)
    return pl.pallas_call(
        functools.partial(cov_kernel, scale),
        grid_spec=pltpu.PrefetchScalarGridSpec(
            num_scalar_prefetch=1,
            grid=(2,),
            in_specs=[
                pl.BlockSpec((1, features, rows), lambda i, s: (2 * s[0] + i, 0, 0)),
                pl.BlockSpec((LAYERS, rows, BG), lambda i, s: (0, 0, 2 * i + s[0])),
            ],
            out_specs=pl.BlockSpec((1,) + shape[1:], lambda i, s: (i, 0, 0, 0, 0)),
            scratch_shapes=[pltpu.VMEM((8, 176, 256), jnp.float32)],
        ),
        out_shape=jax.ShapeDtypeStruct(shape, jnp.float32),
        compiler_params=PARAMS,
        cost_estimate=CHEAP,
        name="covariances",
    )(jnp.stack([core, z]), turned, grads)


def parts_of(x):
    high = x.astype(jnp.bfloat16)
    return high, (x - high.astype(jnp.float32)).astype(jnp.bfloat16)


def times(a, b):
    def one(i, j):
        return jnp.dot(a[i], b[j], preferred_element_type=jnp.float32)

    return (one(0, 1) + one(1, 0)) + one(0, 0)


def roots_kernel(total_ref, packed_ref, wide, square):
    total = total_ref[...]
    spare = pltpu.roll(total[DIAG : DIAG + 1], HALF, 1)
    blocks = [unpack_wide(total[0:RA])[0:BA, 0:BA], unpack_square(total[RA:MSG], spare)]
    eyes, ys, totals = [], [], []
    for c in blocks:
        width = c.shape[0]
        eye = (iota(c.shape, 0) == iota(c.shape, 1)).astype(jnp.float32)
        damped = c + (damping_share * jnp.sum(c * eye) / width) * eye
        trace = jnp.sum(damped * eye)
        eyes.append(eye)
        ys.append(damped / trace)
        totals.append(trace)
    both = range(2)
    zs = [1.5 * eyes[i] - 0.5 * ys[i] for i in both]
    ys = [times(parts_of(ys[i]), parts_of(zs[i])) for i in both]

    def sweep(_, carry):
        ys, zs = carry
        sy, sz = [parts_of(y) for y in ys], [parts_of(z) for z in zs]
        sp = [parts_of(1.5 * eyes[i] - 0.5 * times(sz[i], sy[i])) for i in both]
        return [times(sy[i], sp[i]) for i in both], [times(sp[i], sz[i]) for i in both]

    ys, zs = lax.fori_loop(0, ITERS - 2, sweep, (ys, zs))
    sz = [parts_of(z) for z in zs]
    sp = [parts_of(1.5 * eyes[i] - 0.5 * times(sz[i], parts_of(ys[i]))) for i in both]
    roots = [times(sp[i], sz[i]) / jnp.sqrt(totals[i]) for i in both]
    wide[...] = jnp.zeros_like(wide)
    wide[0:BA, 0:BA] = roots[0]
    square[...], spare = pack_square(roots[1][0:HALF], roots[1][HALF:BG])
    folded, low, corner = pack_wide(wide, spare)
    packed_ref[0:HALF] = folded.astype(jnp.bfloat16)
    packed_ref[HALF:112] = low.astype(jnp.bfloat16)
    packed_ref[112:RA] = corner.astype(jnp.bfloat16)
    start = pl.multiple_of((lax.axis_index("dp") >> 4) * (RG // 2), RG // 2)
    packed_ref[RA:GATHERED] = square[pl.ds(start, RG // 2)].astype(jnp.bfloat16)


def inverse_roots(total):
    whole = pl.BlockSpec(memory_space=pltpu.VMEM)
    return pl.pallas_call(
        roots_kernel,
        in_specs=[whole],
        out_specs=whole,
        out_shape=jax.ShapeDtypeStruct((GATHERED, BG), jnp.bfloat16),
        scratch_shapes=[pltpu.VMEM((176, 256), jnp.float32), pltpu.VMEM((RG, BG), jnp.float32)],
        compiler_params=PARAMS,
        cost_estimate=CHEAP,
        name="inverse_roots",
    )(total)


def unpack_halves(first, second, spare):
    return unpack_square(jnp.concatenate([first, second], axis=0), pltpu.roll(spare, HALF, 1))


def owned_blocks(owners_ref, per_layer, position):
    first = second = jnp.int32(-1)
    for place in range(LAYERS * per_layer):
        mine = owners_ref[place // per_layer, place % per_layer] == position
        second = jnp.where(mine & (first >= 0), place, second)
        first = jnp.where(mine & (first < 0), place, first)
    return first, second


def right_kernel(w_ref, even_ref, odd_ref, mid_ref, right, spares):
    start = source_of(lax.axis_index("dp") >> 2, lax.axis_index("grp"))
    for odd, ref in enumerate((even_ref, odd_ref)):
        for turn in range(4):
            source = ((start ^ odd) - 2 * turn) & 7
            right[source] = ref[32 * turn : 32 * (turn + 1)].astype(jnp.float32)
            spares[source] = ref[128:144].astype(jnp.float32)[turn : turn + 1]
    for layer in range(LAYERS):
        root = unpack_halves(right[layer], right[layer + 4], spares[layer]).astype(jnp.bfloat16)
        product = jnp.dot(w_ref[layer], root, preferred_element_type=jnp.float32)
        mid_ref[layer] = product.astype(jnp.bfloat16).astype(jnp.float32)


def multiply_right(weight_grad, even, odd):
    whole = pl.BlockSpec(memory_space=pltpu.VMEM)
    return pl.pallas_call(
        right_kernel,
        in_specs=[whole] * 3,
        out_specs=whole,
        out_shape=jax.ShapeDtypeStruct(weight_grad.shape, jnp.float32),
        scratch_shapes=[
            pltpu.VMEM((8, RG // 2, BG), jnp.float32),
            pltpu.VMEM((8, 1, BG), jnp.float32),
        ],
        compiler_params=PARAMS,
        cost_estimate=pl.CostEstimate(
            flops=2 * 10**10, bytes_accessed=6 * 10**6, transcendentals=0
        ),
        name="multiply_right",
    )(weight_grad, even, odd)


def apply_kernel(
    oa_ref, og_ref, mid_ref, own_ref, first_ref, rest_ref, out_ref, sa_ref, sg_ref, a_ref
):
    position = lax.axis_index("dp")
    z, y, c = position >> 2, (position >> 1) & 1, position & 1
    owned_a, owned_g = owned_blocks(oa_ref, 8, position), owned_blocks(og_ref, 4, position)

    def place(z_of, y_of, c_of):
        odd = (z ^ z_of) & 1
        turn = (((z ^ odd) - z_of) & 7) >> 1
        return c_of ^ c, 8 * odd + 4 * (y_of ^ y) + turn

    for slot in range(16):
        a_ref[0, slot] = own_ref[GATHERED * slot : GATHERED * (slot + 1)]
        ref, start = (first_ref, slot) if slot < 4 else (rest_ref, slot - 4)
        a_ref[1, slot] = ref[GATHERED * start : GATHERED * (start + 1)]
    for layer in range(LAYERS):
        for quad in range(2):
            results = []
            for k in range(4 * quad, 4 * quad + 4):
                i, slot = place(k, layer % 2, layer // 2)
                left = unpack_wide(a_ref[i, slot, 0:RA].astype(jnp.float32))
                left = left[0:BA, 0:BA].astype(jnp.bfloat16)
                x = mid_ref[layer, BA * k : BA * (k + 1)].astype(jnp.bfloat16)
                results.append(jnp.dot(left, x, preferred_element_type=jnp.float32))
            out_ref[layer, 4 * BA * quad : 4 * BA * (quad + 1)] = jnp.concatenate(
                results, axis=0
            ).astype(jnp.bfloat16)
    stored = []
    for r in range(2):
        block = owned_a[r]
        held = jnp.maximum(block, 0)
        layer = held >> 3
        i, slot = place(held & 7, layer & 1, layer >> 1)
        root = unpack_wide(a_ref[i, slot, 0:RA].astype(jnp.float32))[0:BA, 0:BA]
        stored.append(jnp.where(block >= 0, root, 0.0))
        block = owned_g[r]
        held = jnp.maximum(block, 0)
        layer, k = held >> 2, held & 3
        halves = []
        for half in range(2):
            i, slot = place(layer + 4 * half, k >> 1, k & 1)
            halves.append(a_ref[i, slot, RA - 16 : GATHERED].astype(jnp.float32))
        spare = halves[0][DIAG - RA + 16 : DIAG - RA + 17]
        root = unpack_halves(halves[0][16:48], halves[1][16:48], spare)
        sg_ref[r] = jnp.where(block >= 0, root, 0.0).astype(jnp.bfloat16)
    sa_ref[...] = jnp.stack(stored, axis=1).astype(jnp.bfloat16)


def apply_roots(owner_a, owner_g, mid, *gathered):
    whole = pl.BlockSpec(memory_space=pltpu.VMEM)
    return pl.pallas_call(
        apply_kernel,
        in_specs=[pl.BlockSpec(memory_space=pltpu.SMEM)] * 2 + [whole] * 4,
        out_specs=[whole] * 3,
        out_shape=[
            jax.ShapeDtypeStruct(mid.shape, jnp.bfloat16),
            jax.ShapeDtypeStruct((BA, 2, BA), jnp.bfloat16),
            jax.ShapeDtypeStruct((2, BG, BG), jnp.bfloat16),
        ],
        scratch_shapes=[pltpu.VMEM((2, 16, GATHERED, BG), jnp.bfloat16)],
        compiler_params=PARAMS,
        cost_estimate=CHEAP,
        name="apply_roots",
    )(owner_a, owner_g, mid, *gathered)


def along_z(shift):
    return [(i, (i + 4 * shift) % 32) for i in range(32)]


OVER_CORE = [(i, i ^ 1) for i in range(32)]
OVER_Y = [(i, i ^ 2) for i in range(32)]
OVER_Z = [(i, i ^ 4) for i in range(32)]
OVER_BOTH = [(i, i ^ 6) for i in range(32)]
AWAY = (4, 6, 3, 1, 2, 0, 5, 7)


def source_of(z, g):
    place = 2 * (((g >> 1) - (z >> 1)) & 3) + ((g ^ z) & 1)
    away = sum(jnp.where(place == i, AWAY[i], 0) for i in range(8))
    return (z + away) & 7


def from_column(odd):
    pairs = []
    for z in range(8):
        for g in range(8):
            away = AWAY[2 * ((g // 2 - z // 2) % 4) + (g + z) % 2]
            source = (z + away) % 8 ^ odd
            pairs += [((source * 4 + r) * 8 + z, (z * 4 + r) * 8 + g) for r in range(4)]
    return sorted(pairs)


def tails_of(messages):
    rows = [x[RA:GATHERED] for x in messages] + [x[DIAG : DIAG + 1] for x in messages]
    return jnp.concatenate(rows + [jnp.zeros((12, BG), jnp.bfloat16)])


def narrow(x):
    return (x * WIRE_SCALE).astype(WIRE)


def widen(x):
    return x.astype(jnp.float32) * (1.0 / WIRE_SCALE)


def shards(hidden_acts, out_grads, weight_grad, owner_a, gradient_block_owner):
    position = lax.axis_index("dp")
    z, y, core = position // 4, lax.rem(position // 2, 2), lax.rem(position, 2)
    scale = 1.0 / (hidden_acts.shape[1] * lax.axis_size("dp"))
    turned = jnp.swapaxes(hidden_acts, 1, 2)

    theirs = covariances(turned, out_grads, 1 - core, z, scale)
    got = lax.ppermute(theirs, "dp", OVER_CORE)
    mine = covariances(turned, out_grads, core, z, scale)

    def chip_sum(of_y):
        one = lax.dynamic_index_in_dim(mine, of_y, 0, False)
        return one + lax.dynamic_index_in_dim(got, of_y, 0, False)

    other, own = chip_sum(1 - y), chip_sum(y)
    got_both = lax.ppermute(narrow(other[1]), "dp", OVER_BOTH)
    got_y = lax.ppermute(narrow(other[0]), "dp", OVER_Y)
    got_z = lax.ppermute(narrow(own[1]), "dp", OVER_Z)
    kept = (own[0] + widen(got_y)) + (widen(got_both) + widen(got_z))

    def message(turn):
        start = (turn // 2) * MSG
        return jnp.concatenate(
            [kept[turn % 2, start : start + RA], kept[turn % 2, RA:MSG]], axis=0
        )

    arrived = [lax.ppermute(narrow(message(t)), "dp", along_z(2 * t)) for t in range(1, 4)]
    total = message(0) + sum(widen(x) for x in arrived)
    packed = inverse_roots(total)

    held = [packed] + [lax.ppermute(packed, "dp", along_z(2 * t)) for t in range(1, 4)]
    tails = tails_of(held)
    held = jnp.concatenate(held)
    got_y = lax.ppermute(held, "dp", OVER_Y)
    got_z = lax.ppermute(held, "dp", OVER_Z)
    got_both = lax.ppermute(held, "dp", OVER_BOTH)
    first, tails = lax.optimization_barrier((lax.ppermute(held, "dp", OVER_CORE), tails))
    tails = [lax.ppermute(tails, ("dp", "grp"), pairs) for pairs in map(from_column, (0, 1))]
    gathered = jnp.concatenate([held, got_y, got_z, got_both])
    rest = lax.ppermute(gathered[4 * GATHERED :], "dp", OVER_CORE)

    mid = multiply_right(weight_grad, *tails)
    precond_grad, store_a, store_g = apply_roots(
        owner_a, gradient_block_owner, mid, gathered, first, rest
    )
    return precond_grad, jnp.swapaxes(store_a, 0, 1)[None, None], store_g[None, None]


def solution(mesh):
    return jax.shard_map(
        shards,
        mesh=mesh,
        in_specs=(
            P(None, "dp", "grp"),
            P(None, "dp", "grp"),
            P(None, "grp", "dp"),
            P(None, "grp"),
            P(None, "grp"),
        ),
        out_specs=(
            P(None, "grp", "dp"),
            P("grp", "dp", None, None, None),
            P("grp", "dp", None, None, None),
        ),
        check_vma=False,
    )
```
